128 devices in a mesh: row: 8 (over z_hi, x), col: 16 (over y, z_lo, core).
Axes of the slice: x: 4, y: 4, z: 4 (z_hi: 2, z_lo: 2; z = z_hi * 2 + z_lo), core: 2. Of those that a mesh axis runs over, the one named last changes fastest.
Arguments:
- position: float32 [3, 65536], P(None, ('row', 'col')), may hold values from 0 to 1
- normal: float32 [3, 65536], P(None, ('row', 'col')), may hold values from -1 to 1, as said below
- area: float32 [65536], P(('row', 'col')), may hold values from 0.00061035156 to 0.0061035156
- emission: float32 [32, 65536], P(None, ('row', 'col')), may hold values from 0.05 to 1
- reflect: float32 [32, 65536], P(None, ('row', 'col')), may hold values from 0.3 to 0.95
- pair_list: int32 [8, 16, 128], P('row', 'col'), may hold values from 0 to 511, as said below
- pair_count: int32 [8, 16], P('row', 'col'), may hold values from 32 to 128
- visible: int32 [8, 16, 128, 32, 256], P('row', 'col'), may hold values from 0 to 255
Outputs:
- radiosity: float32 [32, 65536], P(None, ('row', 'col'))
The draws below stay inside these ranges and needn't reach their ends.
Inputs may be any that keep to these rules, and one draw needn't show every extreme that they name: `pair_list`: the 128 codes of one device are distinct. `normal`: unit vectors.
All inputs are finite; a program needn't handle non-finite values.
Results may differ from the reference program's by a relative error of at most 0.0003.
Values sent between devices are 32-bit elements; how exact they have to be, the bound alone decides.
A program may use at most 128 MiB of HBM per device.

```python
import math
import jax
import jax.numpy as jnp
from jax import lax

BLK = 256
WORDS = 32
BANDS = 32
R_DEV = 32
S_DEV = 16
PAIRS_DEV = 128
ITERS = 3
PATCHES = 65536
N_ROW = 8
N_COL = 16


def draw_normal(key, part):
    key = jax.random.fold_in(key, 5)
    first_key, second_key = jax.random.split(key)
    height = jax.random.uniform(first_key, (PATCHES,), jnp.float32, -1.0, 1.0)
    azimuth = jax.random.uniform(second_key, (PATCHES,), jnp.float32, -math.pi, math.pi)
    radial = jnp.sqrt(jnp.maximum(1.0 - height * height, 0.0))
    return jnp.stack([radial * jnp.cos(azimuth), radial * jnp.sin(azimuth), height]).astype(jnp.float32)


def draw_pair_list(key, part):
    key = jax.random.fold_in(key, 7)
    candidates = R_DEV * S_DEV
    devices = N_ROW * N_COL
    scores = jax.random.randint(key, (devices, candidates), 0, 2 ** 30 // candidates, jnp.int32)
    values = jnp.arange(candidates, dtype=jnp.int32)
    ranked = scores * candidates + values[None, :]
    first_device = jnp.where(values == candidates - 1, -2, jnp.where(values == 0, -1, ranked[0]))
    ranked = ranked.at[0].set(first_device)
    ordering = jnp.argsort(ranked, axis=1, stable=True).astype(jnp.int32)
    return ordering[:, :PAIRS_DEV].reshape(N_ROW, N_COL, PAIRS_DEV)


def draw_pair_count(key, part):
    key = jax.random.fold_in(key, 9)
    first_key, second_key, third_key = jax.random.split(key, 3)
    devices = N_ROW * N_COL
    least = PAIRS_DEV // 4
    counts = jax.random.randint(first_key, (devices,), least, PAIRS_DEV + 1, jnp.int32)
    busiest = jax.random.randint(second_key, (), 0, devices, jnp.int32)
    lightest = (busiest + 1 + jax.random.randint(third_key, (), 0, devices - 1, jnp.int32)) % devices
    counts = counts.at[busiest].set(PAIRS_DEV).at[lightest].set(least)
    return counts.reshape(N_ROW, N_COL)


def plant(drawn, rng, low, high):
    longest = drawn.shape.index(max(drawn.shape))
    spots = []
    for shift in (0, 1):
        where = [jax.random.randint(jax.random.fold_in(rng, axis), (), 0, length) for axis, length in enumerate(drawn.shape)]
        where[longest] = (where[longest] + shift) % drawn.shape[longest]
        spots.append(tuple(where))
    return drawn.at[spots[0]].set(low).at[spots[1]].set(high)


def block_levels(stream_key, extent, cuts, low, top_value):
    def one(dim, blocks):
        steps = jax.random.uniform(jax.random.fold_in(jax.random.fold_in(stream_key, 6), dim), (blocks,), jnp.float32, low / len(cuts), top_value / len(cuts))
        return jnp.repeat(jnp.exp(steps), extent[dim] // blocks).reshape((-1,) + (1,) * (len(extent) - dim - 1))

    level = one(*cuts[0])
    for cut in cuts[1:]:
        level = level * one(*cut)
    return level


def setup_inputs(seed: int = 0) -> dict:
    keys = jax.random.split(jax.random.key(seed), 9)
    position = jnp.clip(1.0 * jax.random.uniform(keys[0], (3, PATCHES), jnp.float32) ** block_levels(keys[0], (3, PATCHES), ((1, 128),), -0.2, 0.2), 0.0, 1.0)
    normal = draw_normal(jax.random.fold_in(keys[8], 71), 0)
    area = jnp.clip(jnp.exp(math.log(0.0061035156) - 2.3025851 * jax.random.uniform(keys[2], (PATCHES,), jnp.float32) ** block_levels(keys[2], (PATCHES,), ((0, 128),), -0.2, 0.2)), 0.00061035156, 0.0061035156)
    emission = jnp.clip(jnp.exp(math.log(1.0) - 2.9957323 * jax.random.uniform(keys[3], (BANDS, PATCHES), jnp.float32) ** block_levels(keys[3], (BANDS, PATCHES), ((1, 128),), -0.2, 0.2)), 0.05, 1.0)
    reflect = jnp.clip(0.3 + 0.65 * jax.random.uniform(keys[4], (BANDS, PATCHES), jnp.float32) ** block_levels(keys[4], (BANDS, PATCHES), ((1, 128),), -0.2, 0.2), 0.3, 0.95)
    pair_list = draw_pair_list(jax.random.fold_in(keys[8], 71), 0)
    pair_count = draw_pair_count(jax.random.fold_in(keys[8], 71), 0)
    visible = plant(jax.random.randint(keys[7], (N_ROW, N_COL, PAIRS_DEV, WORDS, BLK), 0, 256), jax.random.fold_in(keys[7], 1), 0, 255).astype(jnp.int32)
    return dict(position=position, normal=normal, area=area, emission=emission, reflect=reflect, pair_list=pair_list, pair_count=pair_count, visible=visible)


def tile_factor(receiver_pos, receiver_nrm, source_pos, source_nrm, source_area, packed_bits):
    shifts = jnp.arange(8, dtype=jnp.int32)
    unpacked = jnp.bitwise_and(jnp.right_shift(packed_bits[:, None, :], shifts[None, :, None]), 1)
    seen_mask = unpacked.reshape(-1, packed_bits.shape[1]).astype(jnp.float32)
    offset_vec = source_pos[:, :, None] - receiver_pos[:, None, :]
    receiver_cos = jnp.maximum(jnp.sum(receiver_nrm[:, None, :] * offset_vec, axis=0), 0.0)
    source_cos = jnp.maximum(-jnp.sum(source_nrm[:, :, None] * offset_vec, axis=0), 0.0)
    spread = jnp.sum(offset_vec * offset_vec, axis=0) + source_area[:, None] / math.pi
    return seen_mask * receiver_cos * source_cos * source_area[:, None] / (math.pi * spread * spread)


def reference(position, normal, area, emission, reflect, pair_list, pair_count, visible):
    quarter = R_DEV // N_COL
    flat_pairs = pair_list.reshape(-1).astype(jnp.int32)
    flat_visible = visible.reshape(-1, WORDS, BLK)
    item_index = jnp.arange(N_ROW * N_COL * PAIRS_DEV, dtype=jnp.int32)
    slot_index = item_index % PAIRS_DEV
    device_index = item_index // PAIRS_DEV
    row_index = device_index // N_COL
    col_index = device_index % N_COL
    live_slot = (slot_index < pair_count.reshape(-1)[device_index]).astype(jnp.float32)
    receiver_block = row_index * R_DEV + flat_pairs // S_DEV
    source_local = flat_pairs % S_DEV
    source_block = (source_local // quarter) * R_DEV + col_index * quarter + source_local % quarter

    def sweep(radiosity):
        outgoing = radiosity

        def add_tile(running, item):
            rec_block, src_block, live_flag, packed_bits = item
            rec_start = (rec_block * BLK).astype(jnp.int32)
            src_start = (src_block * BLK).astype(jnp.int32)
            factor = tile_factor(
                lax.dynamic_slice_in_dim(position, rec_start, BLK, 1),
                lax.dynamic_slice_in_dim(normal, rec_start, BLK, 1),
                lax.dynamic_slice_in_dim(position, src_start, BLK, 1),
                lax.dynamic_slice_in_dim(normal, src_start, BLK, 1),
                lax.dynamic_slice_in_dim(area, src_start, BLK, 0),
                packed_bits)
            contrib = jnp.dot(lax.dynamic_slice_in_dim(outgoing, src_start, BLK, 1), factor,
                              precision=lax.Precision.HIGHEST, preferred_element_type=jnp.float32)
            previous = lax.dynamic_slice_in_dim(running, rec_start, BLK, 1)
            running = lax.dynamic_update_slice_in_dim(running, previous + live_flag * contrib, rec_start, 1)
            return running, None

        start_sum = jnp.zeros((BANDS, PATCHES), jnp.float32)
        gathered, _ = lax.scan(add_tile, start_sum, (receiver_block, source_block, live_slot, flat_visible))
        return gathered

    radiosity = emission
    for sweep_index in range(ITERS):
        radiosity = emission + reflect * sweep(radiosity)
    return radiosity
```

```python
import functools
import math

import jax
import jax.numpy as jnp
from jax import lax
from jax.experimental import pallas as pl
from jax.experimental.pallas import tpu as pltpu
from jax.sharding import PartitionSpec as P

ITERS = 3
MESH = pl.DeviceIdType.MESH
F32, BF16, I32 = jnp.float32, jnp.bfloat16, jnp.int32
CHUNK = 64
SLOT_STEP = 4
SWEEP_STEP = 8


def pieces(x):
    high = x.astype(BF16).astype(F32)
    rest = x - high
    middle = rest.astype(BF16).astype(F32)
    return high, middle, rest - middle


def kernel(
    n_row, n_col, ints, floats, position, normal, area, emission, reflect, visible, out,
    factor_hi, factor_lo, seen_words, running, lhs, rhs, shuffle, turned, own_source, own_receiver,
    own_sent, source_rows, receiver_rows, gathered, outgoing, pair_out, pair_in, mine, peer_in,
    vis_sem, src_send, src_recv, rec_send, rec_recv, out_send, out_recv, pair_send, pair_recv, peer_send, peer_recv,
):
    slots, words, block = visible.shape
    bands, piece = emission.shape
    per_piece = piece // block
    n_chip = n_col // 2
    n_source = per_piece * n_row
    row, col = lax.axis_index("row"), lax.axis_index("col")
    chip, core = col // 2, col % 2

    fetch = pltpu.make_async_copy(visible, seen_words, vis_sem)
    fetch.start()

    centre = position[...] - 0.5
    facing = normal[...]
    weight = area[...] * (1.0 / math.pi)
    along = jnp.sum(facing * centre, axis=0, keepdims=True)
    square = jnp.sum(centre * centre, axis=0, keepdims=True)
    own_source[0:3, :] = centre
    own_source[3:4, :] = square + weight
    own_source[4:7, :] = facing * weight
    own_source[7:8, :] = -along * weight
    own_receiver[0:3, :] = facing
    own_receiver[3:4, :] = -along
    own_receiver[4:7, :] = centre
    own_receiver[7:8, :] = square

    here = lax.broadcasted_iota(I32, (block, block), 0)
    there = lax.broadcasted_iota(I32, (block, block), 1)
    shuffle[...] = jnp.where(here == (there % words) * 8 + there // words, 1.0, 0.0).astype(BF16)

    def shuffled(x, part):
        cut = x[:, part * block : (part + 1) * block]
        stacked = jnp.concatenate([v.astype(BF16) for v in pieces(cut)], axis=0)
        moved = jnp.dot(stacked, shuffle[...], preferred_element_type=F32)
        return moved[:bands] + moved[bands : 2 * bands] + moved[2 * bands :]

    def set_sent(sweep, x):
        for part in range(per_piece):
            own_sent[sweep, :, part * block : (part + 1) * block] = shuffled(x, part)

    set_sent(0, emission[...])

    barrier = pltpu.get_barrier_semaphore()
    for k in range(1, n_row):
        pl.semaphore_signal(barrier, inc=1, device_id=((row + k) % n_row, col), device_id_type=MESH)
    for k in range(1, n_col):
        pl.semaphore_signal(barrier, inc=1, device_id=(row, (col + k) % n_col), device_id_type=MESH)
    pl.semaphore_wait(barrier, n_row + n_col - 2)

    def to_source(k):
        return pltpu.make_async_remote_copy(
            own_source, source_rows.at[k], src_send.at[k], src_recv.at[k],
            device_id=((row + k) % n_row, col), device_id_type=MESH)

    def to_receiver(k):
        return pltpu.make_async_remote_copy(
            own_receiver, receiver_rows.at[k], rec_send.at[k], rec_recv.at[k],
            device_id=(row, (col + k) % n_col), device_id_type=MESH)

    def to_row(sweep, k):
        return pltpu.make_async_remote_copy(
            own_sent.at[sweep], gathered.at[sweep, k], out_send.at[sweep, k], out_recv.at[sweep, k],
            device_id=((row + k) % n_row, col), device_id_type=MESH)

    def to_pair(sweep, k):
        return pltpu.make_async_remote_copy(
            pair_out.at[sweep, k], pair_in.at[sweep, k], pair_send.at[sweep, k], pair_recv.at[sweep, k],
            device_id=(row, chip * 2 + 1 - core), device_id_type=MESH)

    def to_peer(sweep, k):
        return pltpu.make_async_remote_copy(
            mine.at[sweep, k], peer_in.at[sweep, k], peer_send.at[sweep, k], peer_recv.at[sweep, k],
            device_id=(row, ((chip + k) % n_chip) * 2 + core), device_id_type=MESH)

    for k in range(1, n_row):
        to_source(k).start()
    for k in range(1, n_col):
        to_receiver(k).start()
    for k in range(1, n_row):
        to_row(0, k).start()
    source_rows[0] = own_source[...]
    receiver_rows[0] = own_receiver[...]
    for k in range(1, n_row):
        to_source(k).wait_recv()

    sub = lax.broadcasted_iota(I32, (8, block), 0)
    turned[...] = jnp.zeros_like(turned)

    def make_left(k, _):
        owner = (row - k + n_row) % n_row
        for part in range(per_piece):
            h, m, l = pieces(source_rows[k, :, part * block : (part + 1) * block])
            ones = jnp.where(sub < 3, 1.0, 0.0)
            rows = jnp.concatenate([h, h, m, h, l, m, ones, jnp.zeros((72, block), F32)], axis=0)
            turned[...] = rows.T
            for bit in range(8):
                lhs[owner * per_piece + part, bit * words : (bit + 1) * words, :] = (
                    turned[pl.ds(bit, words, stride=8), :].astype(BF16)[:, :64])
        return 0

    lax.fori_loop(0, n_row, make_left, 0)

    for k in range(1, n_col):
        to_receiver(k).wait_recv()

    def make_right(k, _):
        owner = (col - k + n_col) % n_col
        for part in range(per_piece):
            x = receiver_rows[k, :, part * block : (part + 1) * block]
            h, m, l = pieces(x)

            def at(v, row_in, row_out):
                return jnp.where(sub == row_out, pltpu.roll(v, (row_out - row_in) % 8, 0), 0.0)

            def alone(row_in):
                return at(h, row_in, 0) + at(m, row_in, 1) + at(l, row_in, 2)

            zero = jnp.zeros((8, block), F32)
            one_at_7, one_at_3 = jnp.where(sub == 7, 1.0, 0.0), jnp.where(sub == 3, 1.0, 0.0)
            cosine = [jnp.where(sub < 3, v, 0.0) for v in (h, m, l)]
            emitted = [jnp.where((sub > 3) & (sub < 7), v, 0.0) for v in (h, m, l)]
            emitted[0] = emitted[0] + one_at_7
            spread = [jnp.where(sub < 3, pltpu.roll(v, 4, 0) * -2.0, 0.0) for v in (h, m, l)]
            spread[0] = spread[0] + one_at_3
            for n, (v, last) in enumerate(((cosine, alone(3)), (emitted, zero), (spread, alone(7)))):
                full = jnp.concatenate([v[0], v[1], v[0], v[2], v[0], v[1], last, zero], axis=0)
                rhs[owner * per_piece + part, :, n * block : (n + 1) * block] = full.astype(BF16)
        return 0

    lax.fori_loop(0, n_col, make_right, 0)

    fetch.wait()

    def make_factors(step, _):
        for u in range(SLOT_STEP):
            s = step * SLOT_STEP + u
            code = ints[0, s]
            g, h = code // n_source, code % n_source
            for first in range(0, block, CHUNK):
                left = lhs[h, first : first + CHUNK, :]
                met, left_by, spread = (
                    jnp.dot(left, rhs[g, :, n * block : (n + 1) * block], preferred_element_type=F32)
                    for n in range(3))
                bits = range(first // words, (first + CHUNK) // words)
                seen = jnp.concatenate([(seen_words[s] & (1 << bit)) != 0 for bit in bits], axis=0)
                squared = spread * spread
                inverse = pltpu.reciprocal(squared, approx=True)
                inverse = inverse * (2.0 - squared * inverse)
                value = jnp.maximum(met, 0.0) * jnp.maximum(left_by, 0.0) * inverse
                value = jnp.where(seen, value, 0.0)
                high = value.astype(BF16)
                factor_hi[s, first : first + CHUNK, :] = high
                factor_lo[s, first : first + CHUNK, :] = (value - high.astype(F32)).astype(BF16)
        return 0

    lax.fori_loop(0, slots // SLOT_STEP, make_factors, 0)

    for sweep in range(ITERS):
        gathered[sweep, 0] = own_sent[sweep]
        for k in range(1, n_row):
            to_row(sweep, k).wait_recv()

        def split(k, _):
            owner = (row - k + n_row) % n_row
            for part in range(per_piece):
                x = gathered[sweep, k, :, part * block : (part + 1) * block]
                high = x.astype(BF16)
                outgoing[owner * per_piece + part, 0:bands, :] = high
                outgoing[owner * per_piece + part, bands : 2 * bands, :] = (x - high.astype(F32)).astype(BF16)
            return 0

        lax.fori_loop(0, n_row, split, 0)

        def add_slots(step, total):
            for u in range(SWEEP_STEP):
                i = step * SWEEP_STEP + u
                s, h = ints[1, i], ints[2, i]
                left = outgoing[h]
                both = jnp.dot(left, factor_hi[s], preferred_element_type=F32)
                fine = jnp.dot(left[:bands], factor_lo[s], preferred_element_type=F32)
                total = total * floats[0, i] + (both[:bands] + (both[bands:] + fine))
                running[i] = total
            return total

        lax.fori_loop(0, slots // SWEEP_STEP, add_slots, jnp.zeros((bands, block), F32))

        def summed(owner, part):
            g = owner * per_piece + part
            return running[ints[3, g]] * floats[1, g]

        for k in range(n_chip):
            owner = ((chip + k + 1) % n_chip) * 2 + 1 - core
            for part in range(per_piece):
                pair_out[sweep, (k + 1) % n_chip, :, part * block : (part + 1) * block] = summed(owner, part)
            to_pair(sweep, (k + 1) % n_chip).start()
        for k in range(n_chip):
            kk = (k + 1) % n_chip
            owner = ((chip + kk) % n_chip) * 2 + core
            to_pair(sweep, kk).wait_recv()
            for part in range(per_piece):
                lanes = slice(part * block, (part + 1) * block)
                mine[sweep, kk, :, lanes] = summed(owner, part) + pair_in[sweep, kk, :, lanes]
            if kk:
                to_peer(sweep, kk).start()
        total = mine[sweep, 0]
        for k in range(1, n_chip):
            to_peer(sweep, k).wait_recv()
            total = total + peer_in[sweep, k]
        radiosity = emission[...] + reflect[...] * total
        if sweep < ITERS - 1:
            set_sent(sweep + 1, radiosity)
            for k in range(1, n_row):
                to_row(sweep + 1, k).start()
        else:
            out[...] = radiosity

    for k in range(1, n_row):
        to_source(k).wait_send()
    for k in range(1, n_col):
        to_receiver(k).wait_send()
    for sweep in range(ITERS):
        for k in range(1, n_row):
            to_row(sweep, k).wait_send()
        for k in range(n_chip):
            to_pair(sweep, k).wait_send()
        for k in range(1, n_chip):
            to_peer(sweep, k).wait_send()


def slot_order(pair_list, pair_count, n_source, n_receiver):
    codes = pair_list.reshape(-1)
    slots = codes.shape[0]
    slot = jnp.arange(slots, dtype=I32)
    key = jnp.where(slot < pair_count.reshape(()), codes, n_source * n_receiver + slot)
    rank = jnp.sum((key[None, :] < key[:, None]).astype(I32), axis=1)
    hit = rank[None, :] == slot[:, None]
    order = jnp.sum(jnp.where(hit, slot[None, :], 0), axis=1)
    ranked = jnp.sum(jnp.where(hit, key[None, :], 0), axis=1)
    receiver = ranked // n_source
    before = jnp.concatenate([jnp.full((1,), -1, I32), receiver[:-1]])
    block = jnp.arange(slots, dtype=I32)[:, None]
    last = jnp.sum((receiver[None, :] <= block).astype(I32), axis=1) - 1
    any_slot = jnp.any(receiver[None, :] == block, axis=1)
    ints = jnp.stack([codes, order, ranked % n_source, jnp.maximum(last, 0)])
    floats = jnp.stack([(receiver == before).astype(F32), any_slot.astype(F32)])
    return ints, floats


def solution(mesh):
    n_row, n_col = mesh.shape["row"], mesh.shape["col"]

    def body(position, normal, area, emission, reflect, pair_list, pair_count, visible):
        slots, words, block = visible.shape[-3:]
        bands, piece = emission.shape
        per_piece = piece // block
        n_chip = n_col // 2
        n_source, n_receiver = per_piece * n_row, per_piece * n_col
        ints, floats = slot_order(pair_list, pair_count, n_source, n_receiver)
        in_smem = pl.BlockSpec(memory_space=pltpu.SMEM)
        in_vmem = pl.BlockSpec(memory_space=pltpu.VMEM)
        dma = pltpu.SemaphoreType.DMA
        return pl.pallas_call(
            functools.partial(kernel, n_row, n_col),
            out_shape=jax.ShapeDtypeStruct((bands, piece), F32),
            in_specs=[in_smem] * 2 + [in_vmem] * 5 + [pl.BlockSpec(memory_space=pl.ANY)],
            out_specs=in_vmem,
            scratch_shapes=[
                pltpu.VMEM((slots, block, block), BF16),
                pltpu.VMEM((slots, block, block), BF16),
                pltpu.VMEM((slots, words, block), I32),
                pltpu.VMEM((slots, bands, block), F32),
                pltpu.VMEM((n_source, block, 64), BF16),
                pltpu.VMEM((n_receiver, 64, 3 * block), BF16),
                pltpu.VMEM((block, block), BF16),
                pltpu.VMEM((block, 128), F32),
                pltpu.VMEM((8, piece), F32),
                pltpu.VMEM((8, piece), F32),
                pltpu.VMEM((ITERS, bands, piece), F32),
                pltpu.VMEM((n_row, 8, piece), F32),
                pltpu.VMEM((n_col, 8, piece), F32),
                pltpu.VMEM((ITERS, n_row, bands, piece), F32),
                pltpu.VMEM((n_source, 2 * bands, block), BF16),
                pltpu.VMEM((ITERS, n_chip, bands, piece), F32),
                pltpu.VMEM((ITERS, n_chip, bands, piece), F32),
                pltpu.VMEM((ITERS, n_chip, bands, piece), F32),
                pltpu.VMEM((ITERS, n_chip, bands, piece), F32),
                dma,
                dma((n_row,)), dma((n_row,)),
                dma((n_col,)), dma((n_col,)),
                dma((ITERS, n_row)), dma((ITERS, n_row)),
                dma((ITERS, n_chip)), dma((ITERS, n_chip)),
                dma((ITERS, n_chip)), dma((ITERS, n_chip)),
            ],
            compiler_params=pltpu.CompilerParams(
                collective_id=0, has_side_effects=True, vmem_limit_bytes=62 * 2**20),
        )(ints, floats, position, normal, area.reshape(1, piece), emission, reflect,
          visible.reshape(slots, words, block))

    placed = (
        P(None, ("row", "col")),
        P(None, ("row", "col")),
        P(("row", "col")),
        P(None, ("row", "col")),
        P(None, ("row", "col")),
        P("row", "col", None),
        P("row", "col"),
        P("row", "col", None, None, None),
    )
    return jax.shard_map(
        body, mesh=mesh, in_specs=placed, out_specs=P(None, ("row", "col")), check_vma=False
    )
```

```python
import functools
import math

import jax
import jax.numpy as jnp
from jax import lax
from jax.experimental import pallas as pl
from jax.experimental.pallas import tpu as pltpu
from jax.sharding import PartitionSpec as P

ITERS = 3
MESH = pl.DeviceIdType.MESH
F32, BF16, I32 = jnp.float32, jnp.bfloat16, jnp.int32
CHUNK = 64
SLOT_STEP = 16
SWEEP_STEP = 8
PARTS = 2


def pieces(x):
    high = x.astype(BF16).astype(F32)
    rest = x - high
    middle = rest.astype(BF16).astype(F32)
    return high, middle, rest - middle


def kernel(
    n_row, n_col, pair_count, pair_list, position_in, normal_in, area_in, emission_in, reflect_in, visible, out,
    factor_hi, factor_lo, seen_words, running, lhs, rhs, shuffle, turned, own_source, own_receiver,
    own_sent, source_rows, receiver_rows, gathered, outgoing, pair_out, pair_in, mine, peer_in,
    position, normal, area, emission, reflect, codes, table, ints,
    local_sem, table_sem, src_send, src_recv, rec_send, rec_recv, out_send, out_recv, pair_send, pair_recv, peer_send, peer_recv,
):
    slots, words, block = visible.shape
    bands, piece = emission.shape
    per_piece = piece // block
    n_chip = n_col // 2
    n_source, n_receiver = per_piece * n_row, per_piece * n_col
    some = bands // PARTS
    row, col = lax.axis_index("row"), lax.axis_index("col")
    chip, core = col // 2, col % 2

    barrier = pltpu.get_barrier_semaphore()
    for k in range(1, n_row):
        pl.semaphore_signal(barrier, inc=1, device_id=((row + k) % n_row, col), device_id_type=MESH)
    for k in range(1, n_col):
        pl.semaphore_signal(barrier, inc=1, device_id=(row, (col + k) % n_col), device_id_type=MESH)

    fetches = [
        pltpu.make_async_copy(there, here, local_sem.at[n])
        for n, (there, here) in enumerate((
            (position_in, position), (normal_in, normal), (area_in, area), (pair_list, codes),
            (emission_in, emission), (reflect_in, reflect), (visible, seen_words)))
    ]
    for fetch in fetches:
        fetch.start()

    here = lax.broadcasted_iota(I32, (block, block), 0)
    there = lax.broadcasted_iota(I32, (block, block), 1)
    shuffle[...] = jnp.where(here == (there % words) * 8 + there // words, 1.0, 0.0).astype(BF16)

    for fetch in fetches[:3]:
        fetch.wait()

    centre = position[...] - 0.5
    facing = normal[...]
    weight = area[...] * (1.0 / math.pi)
    along = jnp.sum(facing * centre, axis=0, keepdims=True)
    square = jnp.sum(centre * centre, axis=0, keepdims=True)
    own_source[0:3, :] = centre
    own_source[3:4, :] = square + weight
    own_source[4:7, :] = facing * weight
    own_source[7:8, :] = -along * weight
    own_receiver[0:3, :] = facing
    own_receiver[3:4, :] = -along
    own_receiver[4:7, :] = centre
    own_receiver[7:8, :] = square

    def shuffled(x):
        count = x.shape[0]
        cuts = []
        for part in range(per_piece):
            stacked = jnp.concatenate([v.astype(BF16) for v in pieces(x[:, part * block : (part + 1) * block])], axis=0)
            moved = jnp.dot(stacked, shuffle[...], preferred_element_type=F32)
            cuts.append(moved[:count] + moved[count : 2 * count] + moved[2 * count :])
        return jnp.concatenate(cuts, axis=1)

    def lot(q):
        return slice(q * some, (q + 1) * some)

    pl.semaphore_wait(barrier, n_row + n_col - 2)

    def to_source(k):
        return pltpu.make_async_remote_copy(
            own_source, source_rows.at[k], src_send.at[k], src_recv.at[k],
            device_id=((row + k) % n_row, col), device_id_type=MESH)

    def to_receiver(k):
        return pltpu.make_async_remote_copy(
            own_receiver, receiver_rows.at[k], rec_send.at[k], rec_recv.at[k],
            device_id=(row, (col + k) % n_col), device_id_type=MESH)

    def to_row(sweep, q, k):
        return pltpu.make_async_remote_copy(
            own_sent.at[sweep, q], gathered.at[sweep, q, k], out_send.at[sweep, q, k], out_recv.at[sweep, q, k],
            device_id=((row + k) % n_row, col), device_id_type=MESH)

    def to_pair(sweep, q, k):
        return pltpu.make_async_remote_copy(
            pair_out.at[sweep, q, k], pair_in.at[sweep, q, k], pair_send.at[sweep, q, k], pair_recv.at[sweep, q, k],
            device_id=(row, chip * 2 + 1 - core), device_id_type=MESH)

    def to_peer(sweep, q, k):
        return pltpu.make_async_remote_copy(
            mine.at[sweep, q, k], peer_in.at[sweep, q, k], peer_send.at[sweep, q, k], peer_recv.at[sweep, q, k],
            device_id=(row, ((chip + k) % n_chip) * 2 + core), device_id_type=MESH)

    for k in range(1, n_row):
        to_source(k).start()
    for k in range(1, n_col):
        to_receiver(k).start()
    source_rows[0] = own_source[...]
    receiver_rows[0] = own_receiver[...]

    fetches[3].wait()
    below = lax.broadcasted_iota(I32, (slots, slots), 0)
    across = lax.broadcasted_iota(I32, (slots, slots), 1)
    code = codes[...]
    lane = lax.broadcasted_iota(I32, (1, slots), 1)
    key = jnp.where(lane < pair_count[0, 0], code, n_source * n_receiver + lane)
    key_across = jnp.broadcast_to(key, (slots, slots))
    key_below = key_across.T
    rank = jnp.sum((key_below < key_across).astype(I32), axis=0, keepdims=True)
    hit = jnp.broadcast_to(rank, (slots, slots)).T == across
    ranked = jnp.sum(jnp.where(hit, key_below, 0), axis=0, keepdims=True)
    receiver = ranked // n_source
    before = jnp.where(lane == 0, -1, pltpu.roll(receiver, 1, 1))
    table[0:1, :] = code
    table[1:2, :] = jnp.sum(jnp.where(hit, below, 0), axis=0, keepdims=True)
    table[2:3, :] = ranked % n_source
    table[3:4, :] = (receiver == before).astype(I32)
    upto = jnp.sum((key_below // n_source <= across).astype(I32), axis=0, keepdims=True)
    table[4:5, :] = jnp.maximum(upto - 1, 0)
    table[5:6, :] = (jnp.sum((key_below // n_source == across).astype(I32), axis=0, keepdims=True) > 0).astype(I32)
    table[6:8, :] = jnp.zeros((2, slots), I32)
    listing = pltpu.make_async_copy(table, ints, table_sem)
    listing.start()

    fetches[4].wait()
    for q in range(PARTS):
        own_sent[0, q] = shuffled(emission[lot(q), :])
    for k in range(1, n_row):
        to_source(k).wait_recv()

    sub = lax.broadcasted_iota(I32, (8, block), 0)
    turned[...] = jnp.zeros_like(turned)

    def make_left(k, _):
        owner = (row - k + n_row) % n_row
        for part in range(per_piece):
            h, m, l = pieces(source_rows[k, :, part * block : (part + 1) * block])
            ones = jnp.where(sub < 3, 1.0, 0.0)
            rows = jnp.concatenate([h, h, m, h, l, m, ones, jnp.zeros((72, block), F32)], axis=0)
            turned[...] = rows.T
            for bit in range(8):
                lhs[owner * per_piece + part, bit * words : (bit + 1) * words, :] = (
                    turned[pl.ds(bit, words, stride=8), :].astype(BF16)[:, :64])
        return 0

    lax.fori_loop(0, n_row, make_left, 0)

    for k in range(1, n_col):
        to_receiver(k).wait_recv()

    def make_right(k, _):
        owner = (col - k + n_col) % n_col
        for part in range(per_piece):
            x = receiver_rows[k, :, part * block : (part + 1) * block]
            h, m, l = pieces(x)

            def at(v, row_in, row_out):
                return jnp.where(sub == row_out, pltpu.roll(v, (row_out - row_in) % 8, 0), 0.0)

            def alone(row_in):
                return at(h, row_in, 0) + at(m, row_in, 1) + at(l, row_in, 2)

            zero = jnp.zeros((8, block), F32)
            one_at_7, one_at_3 = jnp.where(sub == 7, 1.0, 0.0), jnp.where(sub == 3, 1.0, 0.0)
            cosine = [jnp.where(sub < 3, v, 0.0) for v in (h, m, l)]
            emitted = [jnp.where((sub > 3) & (sub < 7), v, 0.0) for v in (h, m, l)]
            emitted[0] = emitted[0] + one_at_7
            spread = [jnp.where(sub < 3, pltpu.roll(v, 4, 0) * -2.0, 0.0) for v in (h, m, l)]
            spread[0] = spread[0] + one_at_3
            for n, (v, last) in enumerate(((cosine, alone(3)), (emitted, zero), (spread, alone(7)))):
                full = jnp.concatenate([v[0], v[1], v[0], v[2], v[0], v[1], last, zero], axis=0)
                rhs[owner * per_piece + part, :, n * block : (n + 1) * block] = full.astype(BF16)
        return 0

    lax.fori_loop(0, n_col, make_right, 0)

    for q in range(PARTS):
        for k in range(1, n_row):
            to_row(0, q, k).start()
    fetches[5].wait()
    fetches[6].wait()
    listing.wait()

    def make_factors(step, _):
        for u in range(SLOT_STEP):
            s = step * SLOT_STEP + u
            code = ints[0, s]
            g, h = code // n_source, code % n_source
            for first in range(0, block, CHUNK):
                left = lhs[h, first : first + CHUNK, :]
                met, left_by, spread = (
                    jnp.dot(left, rhs[g, :, n * block : (n + 1) * block], preferred_element_type=F32)
                    for n in range(3))
                bits = range(first // words, (first + CHUNK) // words)
                seen = jnp.concatenate([(seen_words[s] & (1 << bit)) != 0 for bit in bits], axis=0)
                squared = spread * spread
                inverse = pltpu.reciprocal(squared, approx=True)
                inverse = inverse * (2.0 - squared * inverse)
                value = jnp.maximum(met, 0.0) * jnp.maximum(left_by, 0.0) * inverse
                value = jnp.where(seen, value, 0.0)
                high = value.astype(BF16)
                factor_hi[s, first : first + CHUNK, :] = high
                factor_lo[s, first : first + CHUNK, :] = (value - high.astype(F32)).astype(BF16)
        return 0

    lax.fori_loop(0, slots // SLOT_STEP, make_factors, 0)

    for sweep in range(ITERS):
        for q in range(PARTS):
            gathered[sweep, q, 0] = own_sent[sweep, q]
            for k in range(1, n_row):
                to_row(sweep, q, k).wait_recv()

            def split(k, _):
                owner = (row - k + n_row) % n_row
                for part in range(per_piece):
                    x = gathered[sweep, q, k, :, part * block : (part + 1) * block]
                    high = x.astype(BF16)
                    at = owner * per_piece + part
                    outgoing[at, q * some : (q + 1) * some, :] = high
                    outgoing[at, bands + q * some : bands + (q + 1) * some, :] = (x - high.astype(F32)).astype(BF16)
                return 0

            lax.fori_loop(0, n_row, split, 0)

        def add_slots(step, total):
            for u in range(SWEEP_STEP):
                i = step * SWEEP_STEP + u
                s, h = ints[1, i], ints[2, i]
                left = outgoing[h]
                both = jnp.dot(left, factor_hi[s], preferred_element_type=F32)
                fine = jnp.dot(left[:bands], factor_lo[s], preferred_element_type=F32)
                total = total * ints[3, i].astype(F32) + (both[:bands] + (both[bands:] + fine))
                running[i] = total
            return total

        lax.fori_loop(0, slots // SWEEP_STEP, add_slots, jnp.zeros((bands, block), F32))

        def summed(owner, part, q):
            g = owner * per_piece + part
            return running[ints[4, g], q * some : (q + 1) * some, :] * ints[5, g].astype(F32)

        order = [k % n_chip for k in range(1, n_chip + 1)]
        for q in range(PARTS):
            for k in order:
                owner = ((chip + k) % n_chip) * 2 + 1 - core
                for part in range(per_piece):
                    pair_out[sweep, q, k, :, part * block : (part + 1) * block] = summed(owner, part, q)
                to_pair(sweep, q, k).start()
        for q in range(PARTS):
            for k in order:
                owner = ((chip + k) % n_chip) * 2 + core
                to_pair(sweep, q, k).wait_recv()
                for part in range(per_piece):
                    lanes = slice(part * block, (part + 1) * block)
                    mine[sweep, q, k, :, lanes] = summed(owner, part, q) + pair_in[sweep, q, k, :, lanes]
                if k:
                    to_peer(sweep, q, k).start()
        for q in range(PARTS):
            total = mine[sweep, q, 0]
            for k in range(1, n_chip):
                to_peer(sweep, q, k).wait_recv()
                total = total + peer_in[sweep, q, k]
            if sweep < ITERS - 1:
                own_sent[sweep + 1, q] = shuffled(emission[lot(q), :] + reflect[lot(q), :] * total)
                for k in range(1, n_row):
                    to_row(sweep + 1, q, k).start()
            else:
                out[lot(q), :] = total

    for k in range(1, n_row):
        to_source(k).wait_send()
    for k in range(1, n_col):
        to_receiver(k).wait_send()
    for sweep in range(ITERS):
        for q in range(PARTS):
            for k in range(1, n_row):
                to_row(sweep, q, k).wait_send()
            for k in range(n_chip):
                to_pair(sweep, q, k).wait_send()
            for k in range(1, n_chip):
                to_peer(sweep, q, k).wait_send()


def solution(mesh):
    n_row, n_col = mesh.shape["row"], mesh.shape["col"]

    def body(position, normal, area, emission, reflect, pair_list, pair_count, visible):
        slots, words, block = visible.shape[-3:]
        bands, piece = emission.shape
        per_piece = piece // block
        n_chip = n_col // 2
        n_source, n_receiver = per_piece * n_row, per_piece * n_col
        in_smem = pl.BlockSpec(memory_space=pltpu.SMEM)
        in_vmem = pl.BlockSpec(memory_space=pltpu.VMEM)
        dma = pltpu.SemaphoreType.DMA
        anywhere = pl.BlockSpec(memory_space=pl.ANY)
        some = bands // PARTS
        gathered = pl.pallas_call(
            functools.partial(kernel, n_row, n_col),
            out_shape=jax.ShapeDtypeStruct((bands, piece), F32),
            in_specs=[in_smem] + [anywhere] * 7,
            out_specs=in_vmem,
            scratch_shapes=[
                pltpu.VMEM((slots, block, block), BF16),
                pltpu.VMEM((slots, block, block), BF16),
                pltpu.VMEM((slots, words, block), I32),
                pltpu.VMEM((slots, bands, block), F32),
                pltpu.VMEM((n_source, block, 64), BF16),
                pltpu.VMEM((n_receiver, 64, 3 * block), BF16),
                pltpu.VMEM((block, block), BF16),
                pltpu.VMEM((block, 128), F32),
                pltpu.VMEM((8, piece), F32),
                pltpu.VMEM((8, piece), F32),
                pltpu.VMEM((ITERS, PARTS, some, piece), F32),
                pltpu.VMEM((n_row, 8, piece), F32),
                pltpu.VMEM((n_col, 8, piece), F32),
                pltpu.VMEM((ITERS, PARTS, n_row, some, piece), F32),
                pltpu.VMEM((n_source, 2 * bands, block), BF16),
                pltpu.VMEM((ITERS, PARTS, n_chip, some, piece), F32),
                pltpu.VMEM((ITERS, PARTS, n_chip, some, piece), F32),
                pltpu.VMEM((ITERS, PARTS, n_chip, some, piece), F32),
                pltpu.VMEM((ITERS, PARTS, n_chip, some, piece), F32),
                pltpu.VMEM((3, piece), F32),
                pltpu.VMEM((3, piece), F32),
                pltpu.VMEM((1, piece), F32),
                pltpu.VMEM((bands, piece), F32),
                pltpu.VMEM((bands, piece), F32),
                pltpu.VMEM((1, slots), I32),
                pltpu.VMEM((8, slots), I32),
                pltpu.SMEM((8, slots), I32),
                dma((7,)),
                dma,
                dma((n_row,)), dma((n_row,)),
                dma((n_col,)), dma((n_col,)),
                dma((ITERS, PARTS, n_row)), dma((ITERS, PARTS, n_row)),
                dma((ITERS, PARTS, n_chip)), dma((ITERS, PARTS, n_chip)),
                dma((ITERS, PARTS, n_chip)), dma((ITERS, PARTS, n_chip)),
            ],
            compiler_params=pltpu.CompilerParams(
                collective_id=0, has_side_effects=True, vmem_limit_bytes=62 * 2**20),
        )(pair_count, pair_list.reshape(1, slots), position, normal, area.reshape(1, piece), emission, reflect,
          visible.reshape(slots, words, block))
        return emission + reflect * gathered

    placed = (
        P(None, ("row", "col")),
        P(None, ("row", "col")),
        P(("row", "col")),
        P(None, ("row", "col")),
        P(None, ("row", "col")),
        P("row", "col", None),
        P("row", "col"),
        P("row", "col", None, None, None),
    )
    return jax.shard_map(
        body, mesh=mesh, in_specs=placed, out_specs=P(None, ("row", "col")), check_vma=False
    )
```

```python
import functools
import math

import jax
import jax.numpy as jnp
from jax import lax
from jax.experimental import pallas as pl
from jax.experimental.pallas import tpu as pltpu
from jax.sharding import PartitionSpec as P

ITERS = 3
MESH = pl.DeviceIdType.MESH
F32, BF16, I32 = jnp.float32, jnp.bfloat16, jnp.int32
CHUNK = 64
SLOT_STEP = 16
SWEEP_STEP = 16
CUTS = (2, 6)
PARTS = 2


def pieces(x):
    high = x.astype(BF16).astype(F32)
    rest = x - high
    middle = rest.astype(BF16).astype(F32)
    return high, middle, rest - middle


def kernel(
    n_row, n_col, pair_count, pair_list, position_in, normal_in, area_in, emission_in, reflect_in, visible, out,
    factor_hi, factor_lo, seen_words, running, lhs, rhs, shuffle, turned, own_source, own_receiver,
    own_sent, source_rows, receiver_rows, gathered, outgoing, pair_out, pair_in, mine, peer_in,
    position, normal, area, emission, reflect, codes, table, ints,
    local_sem, table_sem, geo_send, geo_recv, out_send, out_recv, pair_send, pair_recv, peer_send, peer_recv,
):
    slots, words, block = visible.shape
    bands, piece = emission.shape
    per_piece = piece // block
    n_chip = n_col // 2
    n_source, n_receiver = per_piece * n_row, per_piece * n_col
    some = bands // PARTS
    row, col = lax.axis_index("row"), lax.axis_index("col")
    chip, core = col // 2, col % 2
    n_x, n_zl = n_row // 2, 2
    n_y = n_chip // n_zl
    row_steps = sorted(((a, b) for a in range(2) for b in range(n_x) if a or b), key=lambda s: -(2 * s[0] + min(s[1], n_x - s[1])))
    chip_steps = sorted(((a, b) for a in range(n_y) for b in range(n_zl) if a or b), key=lambda s: -(min(s[0], n_y - s[0]) + s[1]))

    def row_at(k):
        a, b = row_steps[k - 1]
        return ((row // n_x + a) % 2) * n_x + (row % n_x + b) % n_x

    def chip_at(k):
        if k == 0:
            return chip
        a, b = chip_steps[k - 1]
        return ((chip // n_zl + a) % n_y) * n_zl + (chip % n_zl + b) % n_zl

    barrier = pltpu.get_barrier_semaphore()
    for k in range(1, n_row):
        pl.semaphore_signal(barrier, inc=1, device_id=(row_at(k), col), device_id_type=MESH)
    for k in range(1, n_col):
        pl.semaphore_signal(barrier, inc=1, device_id=(row, (col + k) % n_col), device_id_type=MESH)

    fetches = [
        pltpu.make_async_copy(there, here, local_sem.at[n])
        for n, (there, here) in enumerate((
            (position_in, position), (normal_in, normal), (area_in, area), (pair_list, codes),
            (emission_in, emission), (reflect_in, reflect), (visible, seen_words)))
    ]
    for fetch in fetches:
        fetch.start()

    here = lax.broadcasted_iota(I32, (block, block), 0)
    there = lax.broadcasted_iota(I32, (block, block), 1)
    shuffle[...] = jnp.where(here == (there % words) * 8 + there // words, 1.0, 0.0).astype(BF16)

    for fetch in fetches[:3]:
        fetch.wait()

    centre = position[...] - 0.5
    facing = normal[...]
    weight = area[...] * (1.0 / math.pi)
    along = jnp.sum(facing * centre, axis=0, keepdims=True)
    square = jnp.sum(centre * centre, axis=0, keepdims=True)
    own_source[0:3, :] = centre
    own_source[3:4, :] = square + weight
    own_source[4:7, :] = facing * weight
    own_source[7:8, :] = -along * weight
    own_receiver[0:3, :] = facing
    own_receiver[3:4, :] = -along
    own_receiver[4:7, :] = centre
    own_receiver[7:8, :] = square

    def shuffled(x):
        count = x.shape[0]
        cuts = []
        for part in range(per_piece):
            stacked = jnp.concatenate([v.astype(BF16) for v in pieces(x[:, part * block : (part + 1) * block])], axis=0)
            moved = jnp.dot(stacked, shuffle[...], preferred_element_type=F32)
            cuts.append(moved[:count] + moved[count : 2 * count] + moved[2 * count :])
        return jnp.concatenate(cuts, axis=1)

    def lot(q):
        return pl.ds(pl.multiple_of(q * some, some), some)

    pl.semaphore_wait(barrier, n_row + n_col - 2)

    def to_source(k):
        return pltpu.make_async_remote_copy(
            own_source, source_rows.at[row], geo_send.at[0], geo_recv.at[0],
            device_id=(row_at(k), col), device_id_type=MESH)

    def to_receiver(k):
        return pltpu.make_async_remote_copy(
            own_receiver, receiver_rows.at[col], geo_send.at[1], geo_recv.at[1],
            device_id=(row, (col + k) % n_col), device_id_type=MESH)

    def to_row(u, k):
        return pltpu.make_async_remote_copy(
            own_sent.at[u], gathered.at[u, row], out_send.at[u], out_recv.at[u],
            device_id=(row_at(k), col), device_id_type=MESH)

    def to_pair(u):
        return pltpu.make_async_remote_copy(
            pair_out.at[u], pair_in.at[u], pair_send.at[u], pair_recv.at[u],
            device_id=(row, chip * 2 + 1 - core), device_id_type=MESH)

    def to_peer(u, k):
        return pltpu.make_async_remote_copy(
            mine.at[u, k], peer_in.at[u, k], peer_send.at[u], peer_recv.at[u],
            device_id=(row, chip_at(k) * 2 + core), device_id_type=MESH)

    def wait_all(like, sem):
        pltpu.make_async_copy(like, like, sem).wait()

    all_source = source_rows.at[pl.ds(0, n_row - 1)]
    all_receiver = receiver_rows.at[pl.ds(0, n_col - 1)]

    def all_row(u):
        return gathered.at[u, pl.ds(0, n_row - 1)]

    def all_peer(u):
        return peer_in.at[u, pl.ds(1, n_chip - 1)]

    for k in range(1, n_row):
        to_source(k).start()
    for k in range(1, n_col):
        to_receiver(k).start()
    source_rows[row] = own_source[...]
    receiver_rows[col] = own_receiver[...]

    fetches[3].wait()
    below = lax.broadcasted_iota(I32, (slots, slots), 0)
    across = lax.broadcasted_iota(I32, (slots, slots), 1)
    code = codes[...]
    lane = lax.broadcasted_iota(I32, (1, slots), 1)
    key = jnp.where(lane < pair_count[0, 0], code, n_source * n_receiver + lane)
    key_across = jnp.broadcast_to(key, (slots, slots))
    key_below = key_across.T
    rank = jnp.sum((key_below < key_across).astype(I32), axis=0, keepdims=True)
    hit = jnp.broadcast_to(rank, (slots, slots)).T == across
    ranked = jnp.sum(jnp.where(hit, key_below, 0), axis=0, keepdims=True)
    receiver = ranked // n_source
    before = jnp.where(lane == 0, -1, pltpu.roll(receiver, 1, 1))
    table[0:1, :] = code
    table[1:2, :] = jnp.sum(jnp.where(hit, below, 0), axis=0, keepdims=True)
    table[2:3, :] = ranked % n_source
    table[3:4, :] = (receiver == before).astype(I32)
    upto = jnp.sum((key_below // n_source <= across).astype(I32), axis=0, keepdims=True)
    table[4:5, :] = jnp.maximum(upto - 1, 0)
    table[5:6, :] = (jnp.sum((key_below // n_source == across).astype(I32), axis=0, keepdims=True) > 0).astype(I32)
    table[6:8, :] = jnp.zeros((2, slots), I32)
    listing = pltpu.make_async_copy(table, ints, table_sem)
    listing.start()

    fetches[4].wait()
    for q in range(PARTS):
        own_sent[q] = shuffled(emission[lot(q), :])
    wait_all(all_source, geo_recv.at[0])

    sub = lax.broadcasted_iota(I32, (8, block), 0)
    turned[...] = jnp.zeros_like(turned)

    def make_left(owner, _):
        for part in range(per_piece):
            h, m, l = pieces(source_rows[owner, :, part * block : (part + 1) * block])
            ones = jnp.where(sub < 3, 1.0, 0.0)
            rows = jnp.concatenate([h, h, m, h, l, m, ones, jnp.zeros((72, block), F32)], axis=0)
            turned[...] = rows.T
            for bit in range(8):
                lhs[owner * per_piece + part, bit * words : (bit + 1) * words, :] = (
                    turned[pl.ds(bit, words, stride=8), :].astype(BF16)[:, :64])

        return 0

    lax.fori_loop(0, n_row, make_left, 0)

    wait_all(all_receiver, geo_recv.at[1])

    def make_right(owner, _):
        for part in range(per_piece):
            x = receiver_rows[owner, :, part * block : (part + 1) * block]
            h, m, l = pieces(x)

            def at(v, row_in, row_out):
                return jnp.where(sub == row_out, pltpu.roll(v, (row_out - row_in) % 8, 0), 0.0)

            def alone(row_in):
                return at(h, row_in, 0) + at(m, row_in, 1) + at(l, row_in, 2)

            zero = jnp.zeros((8, block), F32)
            one_at_7, one_at_3 = jnp.where(sub == 7, 1.0, 0.0), jnp.where(sub == 3, 1.0, 0.0)
            cosine = [jnp.where(sub < 3, v, 0.0) for v in (h, m, l)]
            emitted = [jnp.where((sub > 3) & (sub < 7), v, 0.0) for v in (h, m, l)]
            emitted[0] = emitted[0] + one_at_7
            spread = [jnp.where(sub < 3, pltpu.roll(v, 4, 0) * -2.0, 0.0) for v in (h, m, l)]
            spread[0] = spread[0] + one_at_3
            for n, (v, last) in enumerate(((cosine, alone(3)), (emitted, zero), (spread, alone(7)))):
                full = jnp.concatenate([v[0], v[1], v[0], v[2], v[0], v[1], last, zero], axis=0)
                rhs[owner * per_piece + part, :, n * block : (n + 1) * block] = full.astype(BF16)
        return 0

    lax.fori_loop(0, n_col, make_right, 0)

    for q in range(PARTS):
        for k in range(1, n_row):
            to_row(q, k).start()
    fetches[5].wait()
    fetches[6].wait()
    listing.wait()

    def make_factors(step, _):
        for u in range(SLOT_STEP):
            s = step * SLOT_STEP + u
            code = ints[0, s]
            g, h = code // n_source, code % n_source
            for first in range(0, block, CHUNK):
                left = lhs[h, first : first + CHUNK, :]
                met, left_by, spread = (
                    jnp.dot(left, rhs[g, :, n * block : (n + 1) * block], preferred_element_type=F32)
                    for n in range(3))
                bits = range(first // words, (first + CHUNK) // words)
                seen = jnp.concatenate([(seen_words[s] & (1 << bit)) != 0 for bit in bits], axis=0)
                squared = spread * spread
                inverse = pltpu.reciprocal(squared, approx=True)
                inverse = inverse * (2.0 - squared * inverse)
                value = jnp.maximum(met, 0.0) * jnp.maximum(left_by, 0.0) * inverse
                value = jnp.where(seen, value, 0.0)
                high = value.astype(BF16)
                factor_hi[s, first : first + CHUNK, :] = high
                factor_lo[s, first : first + CHUNK, :] = (value - high.astype(F32)).astype(BF16)
        return 0

    lax.fori_loop(0, slots // SLOT_STEP, make_factors, 0)

    def receive(u):
        q = u % PARTS
        gathered[u, row] = own_sent[u]
        wait_all(all_row(u), out_recv.at[u])

        def split(owner, _):
            for part in range(per_piece):
                x = gathered[u, owner, :, part * block : (part + 1) * block]
                high = x.astype(BF16)
                outgoing[q, owner * per_piece + part, 0:some, :] = high
                outgoing[q, owner * per_piece + part, some : 2 * some, :] = (x - high.astype(F32)).astype(BF16)
            return 0

        lax.fori_loop(0, n_row, split, 0)

    def add_slots(u, first, last, total):
        q = u % PARTS

        def step(n, total):
            for i in range(SWEEP_STEP):
                i = n * SWEEP_STEP + i
                s, h = ints[1, i], ints[2, i]
                left = outgoing[q, h]
                both = jnp.dot(left, factor_hi[s], preferred_element_type=F32)
                fine = jnp.dot(left[:some], factor_lo[s], preferred_element_type=F32)
                total = total * ints[3, i].astype(F32) + (both[:some] + (both[some:] + fine))
                running[q, i] = total
            return total

        return lax.fori_loop(first, last, step, total)

    def summed(q, owner, part):
        g = owner * per_piece + part
        return running[q, ints[4, g]] * ints[5, g].astype(F32)

    order = [k % n_chip for k in range(1, n_chip + 1)]

    def send_pair(u):
        for k in order:
            owner = chip_at(k) * 2 + 1 - core
            for part in range(per_piece):
                pair_out[u, k, :, part * block : (part + 1) * block] = summed(u % PARTS, owner, part)
        to_pair(u).start()

    def send_peers(u):
        to_pair(u).wait_recv()
        for k in order:
            owner = chip_at(k) * 2 + core
            for part in range(per_piece):
                lanes = slice(part * block, (part + 1) * block)
                mine[u, k, :, lanes] = summed(u % PARTS, owner, part) + pair_in[u, k, :, lanes]
            if k:
                to_peer(u, k).start()

    def gather(u):
        wait_all(all_peer(u), peer_recv.at[u])
        total = mine[u, 0]
        for k in range(1, n_chip):
            total = total + peer_in[u, k]
        return total

    def pass_on(u):
        q = u % PARTS
        own_sent[u + PARTS] = shuffled(emission[lot(q), :] + reflect[lot(q), :] * gather(u))
        for k in range(1, n_row):
            to_row(u + PARTS, k).start()

    steps = slots // SWEEP_STEP
    halves = PARTS * ITERS
    nothing = jnp.zeros((some, block), F32)
    receive(0)
    add_slots(0, 0, steps, nothing)
    send_pair(0)

    def half(u, _):
        send_peers(u - 1)
        receive(u)
        cut = jnp.where(u % PARTS == 0, CUTS[0], CUTS[1])
        total = add_slots(u, 0, cut, nothing)
        pass_on(u - 1)
        add_slots(u, cut, steps, total)
        send_pair(u)
        return 0

    lax.fori_loop(1, halves - 1, half, 0)
    send_peers(halves - 2)
    receive(halves - 1)
    add_slots(halves - 1, 0, steps, nothing)
    send_pair(halves - 1)
    out[lot((halves - 2) % PARTS), :] = gather(halves - 2)
    send_peers(halves - 1)
    out[lot((halves - 1) % PARTS), :] = gather(halves - 1)

    wait_all(all_source, geo_send.at[0])
    wait_all(all_receiver, geo_send.at[1])

    def drain(u, _):
        wait_all(all_row(u), out_send.at[u])
        to_pair(u).wait_send()
        wait_all(all_peer(u), peer_send.at[u])
        return 0

    lax.fori_loop(0, halves, drain, 0)


def solution(mesh):
    n_row, n_col = mesh.shape["row"], mesh.shape["col"]

    def body(position, normal, area, emission, reflect, pair_list, pair_count, visible):
        slots, words, block = visible.shape[-3:]
        bands, piece = emission.shape
        per_piece = piece // block
        n_chip = n_col // 2
        n_source, n_receiver = per_piece * n_row, per_piece * n_col
        in_smem = pl.BlockSpec(memory_space=pltpu.SMEM)
        in_vmem = pl.BlockSpec(memory_space=pltpu.VMEM)
        dma = pltpu.SemaphoreType.DMA
        anywhere = pl.BlockSpec(memory_space=pl.ANY)
        some = bands // PARTS
        gathered = pl.pallas_call(
            functools.partial(kernel, n_row, n_col),
            out_shape=jax.ShapeDtypeStruct((bands, piece), F32),
            in_specs=[in_smem] + [anywhere] * 7,
            out_specs=in_vmem,
            scratch_shapes=[
                pltpu.VMEM((slots, block, block), BF16),
                pltpu.VMEM((slots, block, block), BF16),
                pltpu.VMEM((slots, words, block), I32),
                pltpu.VMEM((PARTS, slots, some, block), F32),
                pltpu.VMEM((n_source, block, 64), BF16),
                pltpu.VMEM((n_receiver, 64, 3 * block), BF16),
                pltpu.VMEM((block, block), BF16),
                pltpu.VMEM((block, 128), F32),
                pltpu.VMEM((8, piece), F32),
                pltpu.VMEM((8, piece), F32),
                pltpu.VMEM((ITERS * PARTS, some, piece), F32),
                pltpu.VMEM((n_row, 8, piece), F32),
                pltpu.VMEM((n_col, 8, piece), F32),
                pltpu.VMEM((ITERS * PARTS, n_row, some, piece), F32),
                pltpu.VMEM((PARTS, n_source, 2 * some, block), BF16),
                pltpu.VMEM((ITERS * PARTS, n_chip, some, piece), F32),
                pltpu.VMEM((ITERS * PARTS, n_chip, some, piece), F32),
                pltpu.VMEM((ITERS * PARTS, n_chip, some, piece), F32),
                pltpu.VMEM((ITERS * PARTS, n_chip, some, piece), F32),
                pltpu.VMEM((3, piece), F32),
                pltpu.VMEM((3, piece), F32),
                pltpu.VMEM((1, piece), F32),
                pltpu.VMEM((bands, piece), F32),
                pltpu.VMEM((bands, piece), F32),
                pltpu.VMEM((1, slots), I32),
                pltpu.VMEM((8, slots), I32),
                pltpu.SMEM((8, slots), I32),
                dma((7,)),
                dma,
                dma((2,)), dma((2,)),
                dma((ITERS * PARTS,)), dma((ITERS * PARTS,)),
                dma((ITERS * PARTS,)), dma((ITERS * PARTS,)),
                dma((ITERS * PARTS,)), dma((ITERS * PARTS,)),
            ],
            compiler_params=pltpu.CompilerParams(
                collective_id=0, has_side_effects=True, vmem_limit_bytes=62 * 2**20),
        )(pair_count, pair_list.reshape(1, slots), position, normal, area.reshape(1, piece), emission, reflect,
          visible.reshape(slots, words, block))
        return emission + reflect * gathered

    placed = (
        P(None, ("row", "col")),
        P(None, ("row", "col")),
        P(("row", "col")),
        P(None, ("row", "col")),
        P(None, ("row", "col")),
        P("row", "col", None),
        P("row", "col"),
        P("row", "col", None, None, None),
    )
    return jax.shard_map(
        body, mesh=mesh, in_specs=placed, out_specs=P(None, ("row", "col")), check_vma=False
    )
```

```python
import functools
import math

import jax
import jax.numpy as jnp
from jax import lax
from jax.experimental import pallas as pl
from jax.experimental.pallas import tpu as pltpu
from jax.sharding import PartitionSpec as P

ITERS = 3
MESH = pl.DeviceIdType.MESH
F32, BF16, I32 = jnp.float32, jnp.bfloat16, jnp.int32
CHUNK = 64
SLOT_STEP = 16
SWEEP_STEP = 32
CUTS = (1, 3)
PARTS = 2


def pieces(x):
    high = x.astype(BF16).astype(F32)
    rest = x - high
    middle = rest.astype(BF16).astype(F32)
    return high, middle, rest - middle


def kernel(
    n_row, n_col, pair_count, pair_list, position_in, normal_in, area_in, emission_in, reflect_in, visible, out,
    factor_hi, factor_lo, seen_words, running, lhs, rhs, shuffle, turned, own_source, own_receiver,
    own_sent, source_rows, receiver_rows, gathered, outgoing, pair_out, pair_in, mine, peer_in,
    position, normal, area, emission, reflect, codes, table, ints,
    local_sem, table_sem, geo_send, geo_recv, out_send, out_recv, pair_send, pair_recv, peer_send, peer_recv,
):
    slots, words, block = visible.shape
    bands, piece = emission.shape
    per_piece = piece // block
    n_chip = n_col // 2
    n_source, n_receiver = per_piece * n_row, per_piece * n_col
    some = bands // PARTS
    row, col = lax.axis_index("row"), lax.axis_index("col")
    chip, core = col // 2, col % 2
    n_x, n_zl = n_row // 2, 2
    n_y = n_chip // n_zl
    row_steps = sorted(((a, b) for a in range(2) for b in range(n_x) if a or b), key=lambda s: -(2 * s[0] + min(s[1], n_x - s[1])))
    chip_steps = sorted(((a, b) for a in range(n_y) for b in range(n_zl) if a or b), key=lambda s: -(min(s[0], n_y - s[0]) + s[1]))

    def row_at(k):
        a, b = row_steps[k - 1]
        return ((row // n_x + a) % 2) * n_x + (row % n_x + b) % n_x

    def chip_at(k):
        if k == 0:
            return chip
        a, b = chip_steps[k - 1]
        return ((chip // n_zl + a) % n_y) * n_zl + (chip % n_zl + b) % n_zl

    barrier = pltpu.get_barrier_semaphore()
    for k in range(1, n_row):
        pl.semaphore_signal(barrier, inc=1, device_id=(row_at(k), col), device_id_type=MESH)
    for k in range(1, n_col):
        pl.semaphore_signal(barrier, inc=1, device_id=(row, (col + k) % n_col), device_id_type=MESH)

    fetches = [
        pltpu.make_async_copy(there, here, local_sem.at[n])
        for n, (there, here) in enumerate((
            (position_in, position), (normal_in, normal), (area_in, area), (pair_list, codes),
            (emission_in, emission), (reflect_in, reflect), (visible, seen_words)))
    ]
    for fetch in fetches:
        fetch.start()

    here = lax.broadcasted_iota(I32, (block, block), 0)
    there = lax.broadcasted_iota(I32, (block, block), 1)
    shuffle[...] = jnp.where(here == (there % words) * 8 + there // words, 1.0, 0.0).astype(BF16)

    for fetch in fetches[:3]:
        fetch.wait()

    centre = position[...] - 0.5
    facing = normal[...]
    weight = area[...] * (1.0 / math.pi)
    along = jnp.sum(facing * centre, axis=0, keepdims=True)
    square = jnp.sum(centre * centre, axis=0, keepdims=True)
    own_source[0:3, :] = centre
    own_source[3:4, :] = square + weight
    own_source[4:7, :] = facing * weight
    own_source[7:8, :] = -along * weight
    own_receiver[0:3, :] = facing
    own_receiver[3:4, :] = -along
    own_receiver[4:7, :] = centre
    own_receiver[7:8, :] = square

    def shuffled(x):
        count = x.shape[0]
        cuts = []
        for part in range(per_piece):
            stacked = jnp.concatenate([v.astype(BF16) for v in pieces(x[:, part * block : (part + 1) * block])], axis=0)
            moved = jnp.dot(stacked, shuffle[...], preferred_element_type=F32)
            cuts.append(moved[:count] + moved[count : 2 * count] + moved[2 * count :])
        return jnp.concatenate(cuts, axis=1)

    def lot(q):
        return pl.ds(pl.multiple_of(q * some, some), some)

    pl.semaphore_wait(barrier, n_row + n_col - 2)

    def to_source(k):
        return pltpu.make_async_remote_copy(
            own_source, source_rows.at[row], geo_send.at[0], geo_recv.at[0],
            device_id=(row_at(k), col), device_id_type=MESH)

    def to_receiver(k):
        return pltpu.make_async_remote_copy(
            own_receiver, receiver_rows.at[col], geo_send.at[1], geo_recv.at[1],
            device_id=(row, (col + k) % n_col), device_id_type=MESH)

    def to_row(u, k):
        return pltpu.make_async_remote_copy(
            own_sent.at[u], gathered.at[u, row], out_send.at[u], out_recv.at[u],
            device_id=(row_at(k), col), device_id_type=MESH)

    def to_pair(u):
        return pltpu.make_async_remote_copy(
            pair_out.at[u], pair_in.at[u], pair_send.at[u], pair_recv.at[u],
            device_id=(row, chip * 2 + 1 - core), device_id_type=MESH)

    def to_peer(u, k):
        return pltpu.make_async_remote_copy(
            mine.at[u, k], peer_in.at[u, k], peer_send.at[u], peer_recv.at[u],
            device_id=(row, chip_at(k) * 2 + core), device_id_type=MESH)

    def wait_all(like, sem):
        pltpu.make_async_copy(like, like, sem).wait()

    all_source = source_rows.at[pl.ds(0, n_row - 1)]
    all_receiver = receiver_rows.at[pl.ds(0, n_col - 1)]

    def all_row(u):
        return gathered.at[u, pl.ds(0, n_row - 1)]

    def all_peer(u):
        return peer_in.at[u, pl.ds(1, n_chip - 1)]

    for k in range(1, n_row):
        to_source(k).start()
    for k in range(1, n_col):
        to_receiver(k).start()
    source_rows[row] = own_source[...]
    receiver_rows[col] = own_receiver[...]

    fetches[3].wait()
    below = lax.broadcasted_iota(I32, (slots, slots), 0)
    across = lax.broadcasted_iota(I32, (slots, slots), 1)
    code = codes[...]
    lane = lax.broadcasted_iota(I32, (1, slots), 1)
    key = jnp.where(lane < pair_count[0, 0], code, n_source * n_receiver + lane)
    key_across = jnp.broadcast_to(key, (slots, slots))
    key_below = key_across.T
    rank = jnp.sum((key_below < key_across).astype(I32), axis=0, keepdims=True)
    hit = jnp.broadcast_to(rank, (slots, slots)).T == across
    ranked = jnp.sum(jnp.where(hit, key_below, 0), axis=0, keepdims=True)
    receiver = ranked // n_source
    before = jnp.where(lane == 0, -1, pltpu.roll(receiver, 1, 1))
    table[0:1, :] = code
    table[1:2, :] = jnp.sum(jnp.where(hit, below, 0), axis=0, keepdims=True)
    table[2:3, :] = ranked % n_source
    table[3:4, :] = (receiver == before).astype(I32)
    upto = jnp.sum((key_below // n_source <= across).astype(I32), axis=0, keepdims=True)
    table[4:5, :] = jnp.maximum(upto - 1, 0)
    table[5:6, :] = (jnp.sum((key_below // n_source == across).astype(I32), axis=0, keepdims=True) > 0).astype(I32)
    table[6:8, :] = jnp.zeros((2, slots), I32)
    listing = pltpu.make_async_copy(table, ints, table_sem)
    listing.start()

    fetches[4].wait()
    for q in range(PARTS):
        own_sent[q] = shuffled(emission[lot(q), :])
    wait_all(all_source, geo_recv.at[0])

    sub = lax.broadcasted_iota(I32, (8, block), 0)
    turned[...] = jnp.zeros_like(turned)

    def make_left(owner, _):
        for part in range(per_piece):
            h, m, l = pieces(source_rows[owner, :, part * block : (part + 1) * block])
            ones = jnp.where(sub < 3, 1.0, 0.0)
            rows = jnp.concatenate([h, h, m, h, l, m, ones, jnp.zeros((72, block), F32)], axis=0)
            turned[part] = rows.T
            for bit in range(8):
                lhs[owner * per_piece + part, bit * words : (bit + 1) * words, :] = (
                    turned[part, pl.ds(bit, words, stride=8), :].astype(BF16)[:, :64])

        return 0

    lax.fori_loop(0, n_row, make_left, 0, unroll=2)

    for q in range(PARTS):
        for k in range(1, n_row):
            to_row(q, k).start()
    wait_all(all_receiver, geo_recv.at[1])

    def make_right(owner, _):
        for part in range(per_piece):
            x = receiver_rows[owner, :, part * block : (part + 1) * block]
            h, m, l = pieces(x)

            def at(v, row_in, row_out):
                return jnp.where(sub == row_out, pltpu.roll(v, (row_out - row_in) % 8, 0), 0.0)

            def alone(row_in):
                return at(h, row_in, 0) + at(m, row_in, 1) + at(l, row_in, 2)

            zero = jnp.zeros((8, block), F32)
            one_at_7, one_at_3 = jnp.where(sub == 7, 1.0, 0.0), jnp.where(sub == 3, 1.0, 0.0)
            cosine = [jnp.where(sub < 3, v, 0.0) for v in (h, m, l)]
            emitted = [jnp.where((sub > 3) & (sub < 7), v, 0.0) for v in (h, m, l)]
            emitted[0] = emitted[0] + one_at_7
            spread = [jnp.where(sub < 3, pltpu.roll(v, 4, 0) * -2.0, 0.0) for v in (h, m, l)]
            spread[0] = spread[0] + one_at_3
            for n, (v, last) in enumerate(((cosine, alone(3)), (emitted, zero), (spread, alone(7)))):
                full = jnp.concatenate([v[0], v[1], v[0], v[2], v[0], v[1], last, zero], axis=0)
                rhs[owner * per_piece + part, :, n * block : (n + 1) * block] = full.astype(BF16)
        return 0

    lax.fori_loop(0, n_col, make_right, 0, unroll=4)

    fetches[5].wait()
    fetches[6].wait()
    listing.wait()

    def make_factors(step, _):
        for u in range(SLOT_STEP):
            s = step * SLOT_STEP + u
            code = ints[0, s]
            g, h = code // n_source, code % n_source
            for first in range(0, block, CHUNK):
                left = lhs[h, first : first + CHUNK, :]
                met, left_by, spread = (
                    jnp.dot(left, rhs[g, :, n * block : (n + 1) * block], preferred_element_type=F32)
                    for n in range(3))
                bits = range(first // words, (first + CHUNK) // words)
                seen = jnp.concatenate([(seen_words[s] & (1 << bit)) != 0 for bit in bits], axis=0)
                squared = spread * spread
                inverse = pltpu.reciprocal(squared, approx=True)
                value = jnp.maximum(met, 0.0) * jnp.maximum(left_by, 0.0) * inverse
                value = jnp.where(seen, value, 0.0)
                high = value.astype(BF16)
                factor_hi[s, first : first + CHUNK, :] = high
                factor_lo[s, first : first + CHUNK, :] = (value - high.astype(F32)).astype(BF16)
        return 0

    lax.fori_loop(0, slots // SLOT_STEP, make_factors, 0)

    def receive(u):
        q = u % PARTS
        gathered[u, row] = own_sent[u]
        wait_all(all_row(u), out_recv.at[u])

        def split(owner, _):
            for part in range(per_piece):
                x = gathered[u, owner, :, part * block : (part + 1) * block]
                high = x.astype(BF16)
                outgoing[q, owner * per_piece + part, 0:some, :] = high
                outgoing[q, owner * per_piece + part, some : 2 * some, :] = (x - high.astype(F32)).astype(BF16)
            return 0

        lax.fori_loop(0, n_row, split, 0)

    def add_slots(u, first, last, total):
        q = u % PARTS

        def step(n, total):
            for i in range(SWEEP_STEP):
                i = n * SWEEP_STEP + i
                s, h = ints[1, i], ints[2, i]
                left = outgoing[q, h]
                both = jnp.dot(left, factor_hi[s], preferred_element_type=F32)
                fine = jnp.dot(left[:some], factor_lo[s], preferred_element_type=F32)
                total = total * ints[3, i].astype(F32) + (both[:some] + (both[some:] + fine))
                running[q, i] = total
            return total

        return lax.fori_loop(first, last, step, total)

    def summed(q, owner, part):
        g = owner * per_piece + part
        return running[q, ints[4, g]] * ints[5, g].astype(F32)

    order = [k % n_chip for k in range(1, n_chip + 1)]

    def send_pair(u):
        for k in order:
            owner = chip_at(k) * 2 + 1 - core
            for part in range(per_piece):
                pair_out[u, k, :, part * block : (part + 1) * block] = summed(u % PARTS, owner, part)
        to_pair(u).start()

    def send_peers(u):
        to_pair(u).wait_recv()
        for k in order:
            owner = chip_at(k) * 2 + core
            for part in range(per_piece):
                lanes = slice(part * block, (part + 1) * block)
                mine[u, k, :, lanes] = summed(u % PARTS, owner, part) + pair_in[u, k, :, lanes]
            if k:
                to_peer(u, k).start()

    def gather(u):
        wait_all(all_peer(u), peer_recv.at[u])
        total = mine[u, 0]
        for k in range(1, n_chip):
            total = total + peer_in[u, k]
        return total

    def pass_on(u):
        q = u % PARTS
        own_sent[u + PARTS] = shuffled(emission[lot(q), :] + reflect[lot(q), :] * gather(u))
        for k in range(1, n_row):
            to_row(u + PARTS, k).start()

    steps = slots // SWEEP_STEP
    halves = PARTS * ITERS
    nothing = jnp.zeros((some, block), F32)
    receive(0)
    add_slots(0, 0, steps, nothing)
    send_pair(0)

    def half(u, _):
        send_peers(u - 1)
        receive(u)
        cut = jnp.where(u % PARTS == 0, CUTS[0], CUTS[1])
        total = add_slots(u, 0, cut, nothing)
        pass_on(u - 1)
        add_slots(u, cut, steps, total)
        send_pair(u)
        return 0

    lax.fori_loop(1, halves - 1, half, 0)
    send_peers(halves - 2)
    receive(halves - 1)
    add_slots(halves - 1, 0, steps, nothing)
    send_pair(halves - 1)
    out[lot((halves - 2) % PARTS), :] = gather(halves - 2)
    send_peers(halves - 1)
    out[lot((halves - 1) % PARTS), :] = gather(halves - 1)

    wait_all(all_source, geo_send.at[0])
    wait_all(all_receiver, geo_send.at[1])

    def drain(u, _):
        wait_all(all_row(u), out_send.at[u])
        to_pair(u).wait_send()
        wait_all(all_peer(u), peer_send.at[u])
        return 0

    lax.fori_loop(0, halves, drain, 0)


def solution(mesh):
    n_row, n_col = mesh.shape["row"], mesh.shape["col"]

    def body(position, normal, area, emission, reflect, pair_list, pair_count, visible):
        slots, words, block = visible.shape[-3:]
        bands, piece = emission.shape
        per_piece = piece // block
        n_chip = n_col // 2
        n_source, n_receiver = per_piece * n_row, per_piece * n_col
        in_smem = pl.BlockSpec(memory_space=pltpu.SMEM)
        in_vmem = pl.BlockSpec(memory_space=pltpu.VMEM)
        dma = pltpu.SemaphoreType.DMA
        anywhere = pl.BlockSpec(memory_space=pl.ANY)
        some = bands // PARTS
        gathered = pl.pallas_call(
            functools.partial(kernel, n_row, n_col),
            out_shape=jax.ShapeDtypeStruct((bands, piece), F32),
            in_specs=[in_smem] + [anywhere] * 7,
            out_specs=in_vmem,
            scratch_shapes=[
                pltpu.VMEM((slots, block, block), BF16),
                pltpu.VMEM((slots, block, block), BF16),
                pltpu.VMEM((slots, words, block), I32),
                pltpu.VMEM((PARTS, slots, some, block), F32),
                pltpu.VMEM((n_source, block, 64), BF16),
                pltpu.VMEM((n_receiver, 64, 3 * block), BF16),
                pltpu.VMEM((block, block), BF16),
                pltpu.VMEM((per_piece, block, 128), F32),
                pltpu.VMEM((8, piece), F32),
                pltpu.VMEM((8, piece), F32),
                pltpu.VMEM((ITERS * PARTS, some, piece), F32),
                pltpu.VMEM((n_row, 8, piece), F32),
                pltpu.VMEM((n_col, 8, piece), F32),
                pltpu.VMEM((ITERS * PARTS, n_row, some, piece), F32),
                pltpu.VMEM((PARTS, n_source, 2 * some, block), BF16),
                pltpu.VMEM((ITERS * PARTS, n_chip, some, piece), F32),
                pltpu.VMEM((ITERS * PARTS, n_chip, some, piece), F32),
                pltpu.VMEM((ITERS * PARTS, n_chip, some, piece), F32),
                pltpu.VMEM((ITERS * PARTS, n_chip, some, piece), F32),
                pltpu.VMEM((3, piece), F32),
                pltpu.VMEM((3, piece), F32),
                pltpu.VMEM((1, piece), F32),
                pltpu.VMEM((bands, piece), F32),
                pltpu.VMEM((bands, piece), F32),
                pltpu.VMEM((1, slots), I32),
                pltpu.VMEM((8, slots), I32),
                pltpu.SMEM((8, slots), I32),
                dma((7,)),
                dma,
                dma((2,)), dma((2,)),
                dma((ITERS * PARTS,)), dma((ITERS * PARTS,)),
                dma((ITERS * PARTS,)), dma((ITERS * PARTS,)),
                dma((ITERS * PARTS,)), dma((ITERS * PARTS,)),
            ],
            compiler_params=pltpu.CompilerParams(
                collective_id=0, has_side_effects=True, vmem_limit_bytes=62 * 2**20),
        )(pair_count, pair_list.reshape(1, slots), position, normal, area.reshape(1, piece), emission, reflect,
          visible.reshape(slots, words, block))
        return emission + reflect * gathered

    placed = (
        P(None, ("row", "col")),
        P(None, ("row", "col")),
        P(("row", "col")),
        P(None, ("row", "col")),
        P(None, ("row", "col")),
        P("row", "col", None),
        P("row", "col"),
        P("row", "col", None, None, None),
    )
    return jax.shard_map(
        body, mesh=mesh, in_specs=placed, out_specs=P(None, ("row", "col")), check_vma=False
    )
```

```python
import functools
import math

import jax
import jax.numpy as jnp
from jax import lax
from jax.experimental import pallas as pl
from jax.experimental.pallas import tpu as pltpu
from jax.sharding import PartitionSpec as P

ITERS = 3
MESH = pl.DeviceIdType.MESH
F32, BF16, I32 = jnp.float32, jnp.bfloat16, jnp.int32
CHUNK = 64
SLOT_STEP = 16
SWEEP_STEP = 32
CUTS = (1, 3)
PARTS = 2


def pieces(x):
    high = x.astype(BF16).astype(F32)
    rest = x - high
    middle = rest.astype(BF16).astype(F32)
    return high, middle, rest - middle


def kernel(
    n_row, n_col, pair_count, pair_list, position_in, normal_in, area_in, emission_in, reflect_in, visible, out,
    factor_hi, factor_lo, seen_words, running, lhs, rhs, shuffle, turned, own_source, own_receiver,
    own_sent, source_rows, receiver_rows, gathered, outgoing, pair_out, pair_in, mine, peer_in,
    position, normal, area, emission, reflect, codes, table, ints,
    local_sem, table_sem, geo_send, geo_recv, out_send, out_recv, pair_send, pair_recv, peer_send, peer_recv,
):
    slots, words, block = visible.shape
    bands, piece = emission.shape
    per_piece = piece // block
    n_chip = n_col // 2
    n_source, n_receiver = per_piece * n_row, per_piece * n_col
    some = bands // PARTS
    row, col = lax.axis_index("row"), lax.axis_index("col")
    chip, core = col // 2, col % 2
    n_x, n_zl = n_row // 2, 2
    n_y = n_chip // n_zl
    row_steps = sorted(((a, b) for a in range(2) for b in range(n_x) if a or b), key=lambda s: -(2 * s[0] + min(s[1], n_x - s[1])))
    chip_steps = sorted(((a, b) for a in range(n_y) for b in range(n_zl) if a or b), key=lambda s: -(min(s[0], n_y - s[0]) + s[1]))

    def row_at(k):
        a, b = row_steps[k - 1]
        return ((row // n_x + a) % 2) * n_x + (row % n_x + b) % n_x

    def chip_at(k):
        if k == 0:
            return chip
        a, b = chip_steps[k - 1]
        return ((chip // n_zl + a) % n_y) * n_zl + (chip % n_zl + b) % n_zl

    barrier = pltpu.get_barrier_semaphore()
    for k in range(1, n_row):
        pl.semaphore_signal(barrier, inc=1, device_id=(row_at(k), col), device_id_type=MESH)
    for k in range(1, n_col):
        pl.semaphore_signal(barrier, inc=1, device_id=(row, (col + k) % n_col), device_id_type=MESH)

    fetches = [
        pltpu.make_async_copy(there, here, local_sem.at[n])
        for n, (there, here) in enumerate((
            (position_in, position), (normal_in, normal), (area_in, area), (pair_list, codes),
            (emission_in, emission), (reflect_in, reflect), (visible, seen_words)))
    ]
    for fetch in fetches:
        fetch.start()

    here = lax.broadcasted_iota(I32, (block, block), 0)
    there = lax.broadcasted_iota(I32, (block, block), 1)
    shuffle[...] = jnp.where(here == (there % words) * 8 + there // words, 1.0, 0.0).astype(BF16)

    for fetch in fetches[:3]:
        fetch.wait()

    centre = position[...] - 0.5
    facing = normal[...]
    weight = area[...] * (1.0 / math.pi)
    along = jnp.sum(facing * centre, axis=0, keepdims=True)
    square = jnp.sum(centre * centre, axis=0, keepdims=True)
    own_source[0:3, :] = centre
    own_source[3:4, :] = square + weight
    own_source[4:7, :] = facing * weight
    own_source[7:8, :] = -along * weight
    own_receiver[0:3, :] = facing
    own_receiver[3:4, :] = -along
    own_receiver[4:7, :] = centre
    own_receiver[7:8, :] = square

    def shuffled(x):
        count = x.shape[0]
        cuts = []
        for part in range(per_piece):
            stacked = jnp.concatenate([v.astype(BF16) for v in pieces(x[:, part * block : (part + 1) * block])], axis=0)
            moved = jnp.dot(stacked, shuffle[...], preferred_element_type=F32)
            cuts.append(moved[:count] + moved[count : 2 * count] + moved[2 * count :])
        return jnp.concatenate(cuts, axis=1)

    def lot(q):
        return pl.ds(pl.multiple_of(q * some, some), some)

    pl.semaphore_wait(barrier, n_row + n_col - 2)

    def to_source(k):
        return pltpu.make_async_remote_copy(
            own_source, source_rows.at[row], geo_send.at[0], geo_recv.at[0],
            device_id=(row_at(k), col), device_id_type=MESH)

    def to_receiver(k):
        return pltpu.make_async_remote_copy(
            own_receiver, receiver_rows.at[col], geo_send.at[1], geo_recv.at[1],
            device_id=(row, (col + k) % n_col), device_id_type=MESH)

    def to_row(u, k):
        return pltpu.make_async_remote_copy(
            own_sent.at[u], gathered.at[u, row], out_send.at[u], out_recv.at[u],
            device_id=(row_at(k), col), device_id_type=MESH)

    def to_pair(u, lot):
        first = pl.ds(lot * (n_chip // 2), n_chip // 2)
        return pltpu.make_async_remote_copy(
            pair_out.at[u, first], pair_in.at[u, first], pair_send.at[u, lot], pair_recv.at[u, lot],
            device_id=(row, chip * 2 + 1 - core), device_id_type=MESH)

    def to_peer(u, k):
        return pltpu.make_async_remote_copy(
            mine.at[u, k], peer_in.at[u, k], peer_send.at[u], peer_recv.at[u],
            device_id=(row, chip_at(k) * 2 + core), device_id_type=MESH)

    def wait_all(like, sem):
        pltpu.make_async_copy(like, like, sem).wait()

    all_source = source_rows.at[pl.ds(0, n_row - 1)]
    all_receiver = receiver_rows.at[pl.ds(0, n_col - 1)]

    def all_row(u):
        return gathered.at[u, pl.ds(0, n_row - 1)]

    def all_peer(u):
        return peer_in.at[u, pl.ds(1, n_chip - 1)]

    for k in range(1, n_row):
        to_source(k).start()
    for k in range(1, n_col):
        to_receiver(k).start()
    source_rows[row] = own_source[...]
    receiver_rows[col] = own_receiver[...]

    fetches[3].wait()
    below = lax.broadcasted_iota(I32, (slots, slots), 0)
    across = lax.broadcasted_iota(I32, (slots, slots), 1)
    code = codes[...]
    lane = lax.broadcasted_iota(I32, (1, slots), 1)
    key = jnp.where(lane < pair_count[0, 0], code, n_source * n_receiver + lane)
    key_across = jnp.broadcast_to(key, (slots, slots))
    key_below = key_across.T
    rank = jnp.sum((key_below < key_across).astype(I32), axis=0, keepdims=True)
    hit = jnp.broadcast_to(rank, (slots, slots)).T == across
    ranked = jnp.sum(jnp.where(hit, key_below, 0), axis=0, keepdims=True)
    receiver = ranked // n_source
    before = jnp.where(lane == 0, -1, pltpu.roll(receiver, 1, 1))
    table[0:1, :] = code
    table[1:2, :] = jnp.sum(jnp.where(hit, below, 0), axis=0, keepdims=True)
    table[2:3, :] = ranked % n_source
    table[3:4, :] = (receiver == before).astype(I32)
    upto = jnp.sum((key_below // n_source <= across).astype(I32), axis=0, keepdims=True)
    table[4:5, :] = jnp.maximum(upto - 1, 0)
    table[5:6, :] = (jnp.sum((key_below // n_source == across).astype(I32), axis=0, keepdims=True) > 0).astype(I32)
    table[6:8, :] = jnp.zeros((2, slots), I32)
    listing = pltpu.make_async_copy(table, ints, table_sem)
    listing.start()

    fetches[4].wait()
    for q in range(PARTS):
        own_sent[q] = shuffled(emission[lot(q), :])
    wait_all(all_source, geo_recv.at[0])

    sub = lax.broadcasted_iota(I32, (8, block), 0)
    turned[...] = jnp.zeros_like(turned)

    def make_left(owner, _):
        for part in range(per_piece):
            h, m, l = pieces(source_rows[owner, :, part * block : (part + 1) * block])
            ones = jnp.where(sub < 3, 1.0, 0.0)
            rows = jnp.concatenate([h, h, m, h, l, m, ones, jnp.zeros((72, block), F32)], axis=0)
            turned[part] = rows.T
            for bit in range(8):
                lhs[owner * per_piece + part, bit * words : (bit + 1) * words, :] = (
                    turned[part, pl.ds(bit, words, stride=8), :].astype(BF16)[:, :64])

        return 0

    lax.fori_loop(0, n_row, make_left, 0, unroll=2)

    for q in range(PARTS):
        for k in range(1, n_row):
            to_row(q, k).start()
    wait_all(all_receiver, geo_recv.at[1])

    def make_right(owner, _):
        for part in range(per_piece):
            x = receiver_rows[owner, :, part * block : (part + 1) * block]
            h, m, l = pieces(x)

            def at(v, row_in, row_out):
                return jnp.where(sub == row_out, pltpu.roll(v, (row_out - row_in) % 8, 0), 0.0)

            def alone(row_in):
                return at(h, row_in, 0) + at(m, row_in, 1) + at(l, row_in, 2)

            zero = jnp.zeros((8, block), F32)
            one_at_7, one_at_3 = jnp.where(sub == 7, 1.0, 0.0), jnp.where(sub == 3, 1.0, 0.0)
            cosine = [jnp.where(sub < 3, v, 0.0) for v in (h, m, l)]
            emitted = [jnp.where((sub > 3) & (sub < 7), v, 0.0) for v in (h, m, l)]
            emitted[0] = emitted[0] + one_at_7
            spread = [jnp.where(sub < 3, pltpu.roll(v, 4, 0) * -2.0, 0.0) for v in (h, m, l)]
            spread[0] = spread[0] + one_at_3
            for n, (v, last) in enumerate(((cosine, alone(3)), (emitted, zero), (spread, alone(7)))):
                full = jnp.concatenate([v[0], v[1], v[0], v[2], v[0], v[1], last, zero], axis=0)
                rhs[owner * per_piece + part, :, n * block : (n + 1) * block] = full.astype(BF16)
        return 0

    lax.fori_loop(0, n_col, make_right, 0, unroll=4)

    fetches[5].wait()
    fetches[6].wait()
    listing.wait()

    def make_factors(step, _):
        for u in range(SLOT_STEP):
            s = step * SLOT_STEP + u
            code = ints[0, s]
            g, h = code // n_source, code % n_source
            for first in range(0, block, CHUNK):
                left = lhs[h, first : first + CHUNK, :]
                met, left_by, spread = (
                    jnp.dot(left, rhs[g, :, n * block : (n + 1) * block], preferred_element_type=F32)
                    for n in range(3))
                bits = range(first // words, (first + CHUNK) // words)
                seen = jnp.concatenate([(seen_words[s] & (1 << bit)) != 0 for bit in bits], axis=0)
                squared = spread * spread
                inverse = pltpu.reciprocal(squared, approx=True)
                value = jnp.maximum(met, 0.0) * jnp.maximum(left_by, 0.0) * inverse
                value = jnp.where(seen, value, 0.0)
                high = value.astype(BF16)
                factor_hi[s, first : first + CHUNK, :] = high
                factor_lo[s, first : first + CHUNK, :] = (value - high.astype(F32)).astype(BF16)
        return 0

    lax.fori_loop(0, slots // SLOT_STEP, make_factors, 0)

    def receive(u):
        q = u % PARTS
        gathered[u, row] = own_sent[u]
        wait_all(all_row(u), out_recv.at[u])

        def split(owner, _):
            for part in range(per_piece):
                x = gathered[u, owner, :, part * block : (part + 1) * block]
                high = x.astype(BF16)
                outgoing[q, owner * per_piece + part, 0:some, :] = high
                outgoing[q, owner * per_piece + part, some : 2 * some, :] = (x - high.astype(F32)).astype(BF16)
            return 0

        lax.fori_loop(0, n_row, split, 0, unroll=True)

    def add_slots(u, first, last, total):
        q = u % PARTS

        def step(n, total):
            for i in range(SWEEP_STEP):
                i = n * SWEEP_STEP + i
                s, h = ints[1, i], ints[2, i]
                left = outgoing[q, h]
                both = jnp.dot(left, factor_hi[s], preferred_element_type=F32)
                fine = jnp.dot(left[:some], factor_lo[s], preferred_element_type=F32)
                total = total * ints[3, i].astype(F32) + (both[:some] + (both[some:] + fine))
                running[q, i] = total
            return total

        return lax.fori_loop(first, last, step, total)

    def summed(q, owner, part):
        g = owner * per_piece + part
        return running[q, ints[4, g]] * ints[5, g].astype(F32)

    order = [k % n_chip for k in range(1, n_chip + 1)]

    def send_pair(u):
        for k in order:
            owner = chip_at(k) * 2 + 1 - core
            for part in range(per_piece):
                pair_out[u, (k - 1) % n_chip, :, part * block : (part + 1) * block] = summed(u % PARTS, owner, part)
            if k == n_chip // 2:
                to_pair(u, 0).start()
        to_pair(u, 1).start()

    def send_peers(u):
        to_pair(u, 0).wait_recv()
        for k in order:
            if k == n_chip // 2 + 1:
                to_pair(u, 1).wait_recv()
            owner = chip_at(k) * 2 + core
            for part in range(per_piece):
                lanes = slice(part * block, (part + 1) * block)
                mine[u, k, :, lanes] = summed(u % PARTS, owner, part) + pair_in[u, (k - 1) % n_chip, :, lanes]
            if k:
                to_peer(u, k).start()

    def gather(u):
        wait_all(all_peer(u), peer_recv.at[u])
        total = mine[u, 0]
        for k in range(1, n_chip):
            total = total + peer_in[u, k]
        return total

    def pass_on(u):
        q = u % PARTS
        own_sent[u + PARTS] = shuffled(emission[lot(q), :] + reflect[lot(q), :] * gather(u))
        for k in range(1, n_row):
            to_row(u + PARTS, k).start()

    steps = slots // SWEEP_STEP
    halves = PARTS * ITERS
    nothing = jnp.zeros((some, block), F32)
    receive(0)
    add_slots(0, 0, steps, nothing)
    send_pair(0)

    def half(u, _):
        send_peers(u - 1)
        receive(u)
        cut = jnp.where(u % PARTS == 0, CUTS[0], CUTS[1])
        total = add_slots(u, 0, cut, nothing)
        pass_on(u - 1)
        add_slots(u, cut, steps, total)
        send_pair(u)
        return 0

    lax.fori_loop(1, halves - 1, half, 0)
    send_peers(halves - 2)
    receive(halves - 1)
    add_slots(halves - 1, 0, steps, nothing)
    send_pair(halves - 1)
    out[lot((halves - 2) % PARTS), :] = gather(halves - 2)
    send_peers(halves - 1)
    out[lot((halves - 1) % PARTS), :] = gather(halves - 1)

    wait_all(all_source, geo_send.at[0])
    wait_all(all_receiver, geo_send.at[1])

    def drain(u, _):
        wait_all(all_row(u), out_send.at[u])
        to_pair(u, 0).wait_send()
        to_pair(u, 1).wait_send()
        wait_all(all_peer(u), peer_send.at[u])
        return 0

    lax.fori_loop(0, halves, drain, 0)


def solution(mesh):
    n_row, n_col = mesh.shape["row"], mesh.shape["col"]

    def body(position, normal, area, emission, reflect, pair_list, pair_count, visible):
        slots, words, block = visible.shape[-3:]
        bands, piece = emission.shape
        per_piece = piece // block
        n_chip = n_col // 2
        n_source, n_receiver = per_piece * n_row, per_piece * n_col
        in_smem = pl.BlockSpec(memory_space=pltpu.SMEM)
        in_vmem = pl.BlockSpec(memory_space=pltpu.VMEM)
        dma = pltpu.SemaphoreType.DMA
        anywhere = pl.BlockSpec(memory_space=pl.ANY)
        some = bands // PARTS
        gathered = pl.pallas_call(
            functools.partial(kernel, n_row, n_col),
            out_shape=jax.ShapeDtypeStruct((bands, piece), F32),
            in_specs=[in_smem] + [anywhere] * 7,
            out_specs=in_vmem,
            scratch_shapes=[
                pltpu.VMEM((slots, block, block), BF16),
                pltpu.VMEM((slots, block, block), BF16),
                pltpu.VMEM((slots, words, block), I32),
                pltpu.VMEM((PARTS, slots, some, block), F32),
                pltpu.VMEM((n_source, block, 64), BF16),
                pltpu.VMEM((n_receiver, 64, 3 * block), BF16),
                pltpu.VMEM((block, block), BF16),
                pltpu.VMEM((per_piece, block, 128), F32),
                pltpu.VMEM((8, piece), F32),
                pltpu.VMEM((8, piece), F32),
                pltpu.VMEM((ITERS * PARTS, some, piece), F32),
                pltpu.VMEM((n_row, 8, piece), F32),
                pltpu.VMEM((n_col, 8, piece), F32),
                pltpu.VMEM((ITERS * PARTS, n_row, some, piece), F32),
                pltpu.VMEM((PARTS, n_source, 2 * some, block), BF16),
                pltpu.VMEM((ITERS * PARTS, n_chip, some, piece), F32),
                pltpu.VMEM((ITERS * PARTS, n_chip, some, piece), F32),
                pltpu.VMEM((ITERS * PARTS, n_chip, some, piece), F32),
                pltpu.VMEM((ITERS * PARTS, n_chip, some, piece), F32),
                pltpu.VMEM((3, piece), F32),
                pltpu.VMEM((3, piece), F32),
                pltpu.VMEM((1, piece), F32),
                pltpu.VMEM((bands, piece), F32),
                pltpu.VMEM((bands, piece), F32),
                pltpu.VMEM((1, slots), I32),
                pltpu.VMEM((8, slots), I32),
                pltpu.SMEM((8, slots), I32),
                dma((7,)),
                dma,
                dma((2,)), dma((2,)),
                dma((ITERS * PARTS,)), dma((ITERS * PARTS,)),
                dma((ITERS * PARTS, 2)), dma((ITERS * PARTS, 2)),
                dma((ITERS * PARTS,)), dma((ITERS * PARTS,)),
            ],
            compiler_params=pltpu.CompilerParams(
                collective_id=0, has_side_effects=True, vmem_limit_bytes=62 * 2**20),
        )(pair_count, pair_list.reshape(1, slots), position, normal, area.reshape(1, piece), emission, reflect,
          visible.reshape(slots, words, block))
        return emission + reflect * gathered

    placed = (
        P(None, ("row", "col")),
        P(None, ("row", "col")),
        P(("row", "col")),
        P(None, ("row", "col")),
        P(None, ("row", "col")),
        P("row", "col", None),
        P("row", "col"),
        P("row", "col", None, None, None),
    )
    return jax.shard_map(
        body, mesh=mesh, in_specs=placed, out_specs=P(None, ("row", "col")), check_vma=False
    )
```

```python
import functools
import math

import jax
import jax.numpy as jnp
from jax import lax
from jax.experimental import pallas as pl
from jax.experimental.pallas import tpu as pltpu
from jax.sharding import PartitionSpec as P

ITERS = 3
MESH = pl.DeviceIdType.MESH
F32, BF16, I32 = jnp.float32, jnp.bfloat16, jnp.int32
CHUNK = 64
SLOT_STEP = 16
SWEEP_STEP = 32
CUTS = (1, 3)
PARTS = 2


def pieces(x):
    high = x.astype(BF16).astype(F32)
    rest = x - high
    middle = rest.astype(BF16).astype(F32)
    return high, middle, rest - middle


def kernel(
    n_row, n_col, pair_count, pair_list, position_in, normal_in, area_in, emission_in, reflect_in, visible, out,
    factor_hi, factor_lo, seen_words, running, lhs, rhs, shuffle, turned, own_source, own_receiver,
    own_sent, source_rows, receiver_rows, gathered, outgoing, pair_out, pair_in, mine, peer_in,
    position, normal, area, emission, reflect, codes, table, ints,
    local_sem, table_sem, geo_send, geo_recv, out_send, out_recv, pair_send, pair_recv, peer_send, peer_recv,
):
    slots, words, block = visible.shape
    bands, piece = emission.shape
    per_piece = piece // block
    n_chip = n_col // 2
    n_source, n_receiver = per_piece * n_row, per_piece * n_col
    some = bands // PARTS
    row, col = lax.axis_index("row"), lax.axis_index("col")
    chip, core = col // 2, col % 2
    n_x, n_zl = n_row // 2, 2
    n_y = n_chip // n_zl
    row_steps = sorted(((a, b) for a in range(2) for b in range(n_x) if a or b), key=lambda s: -(2 * s[0] + min(s[1], n_x - s[1])))
    chip_steps = sorted(((a, b) for a in range(n_y) for b in range(n_zl) if a or b), key=lambda s: -(min(s[0], n_y - s[0]) + s[1]))

    def row_at(k):
        a, b = row_steps[k - 1]
        return ((row // n_x + a) % 2) * n_x + (row % n_x + b) % n_x

    def chip_at(k):
        if k == 0:
            return chip
        a, b = chip_steps[k - 1]
        return ((chip // n_zl + a) % n_y) * n_zl + (chip % n_zl + b) % n_zl

    barrier = pltpu.get_barrier_semaphore()
    for k in range(1, n_row):
        pl.semaphore_signal(barrier, inc=1, device_id=(row_at(k), col), device_id_type=MESH)
    for k in range(1, n_col):
        pl.semaphore_signal(barrier, inc=1, device_id=(row, (col + k) % n_col), device_id_type=MESH)

    fetches = [
        pltpu.make_async_copy(there, here, local_sem.at[n])
        for n, (there, here) in enumerate((
            (position_in, position), (normal_in, normal), (area_in, area), (pair_list, codes),
            (emission_in, emission), (reflect_in, reflect), (visible, seen_words)))
    ]
    for fetch in fetches:
        fetch.start()

    here = lax.broadcasted_iota(I32, (block, block), 0)
    there = lax.broadcasted_iota(I32, (block, block), 1)
    shuffle[...] = jnp.where(here == (there % words) * 8 + there // words, 1.0, 0.0).astype(BF16)

    for fetch in fetches[:3]:
        fetch.wait()

    centre = position[...] - 0.5
    facing = normal[...]
    weight = area[...] * (1.0 / math.pi)
    along = jnp.sum(facing * centre, axis=0, keepdims=True)
    square = jnp.sum(centre * centre, axis=0, keepdims=True)
    own_source[0:3, :] = centre
    own_source[3:4, :] = square + weight
    own_source[4:7, :] = facing * weight
    own_source[7:8, :] = -along * weight
    own_receiver[0:3, :] = facing
    own_receiver[3:4, :] = -along
    own_receiver[4:7, :] = centre
    own_receiver[7:8, :] = square

    def shuffled(x):
        count = x.shape[0]
        cuts = []
        for part in range(per_piece):
            stacked = jnp.concatenate([v.astype(BF16) for v in pieces(x[:, part * block : (part + 1) * block])], axis=0)
            moved = jnp.dot(stacked, shuffle[...], preferred_element_type=F32)
            cuts.append(moved[:count] + moved[count : 2 * count] + moved[2 * count :])
        return jnp.concatenate(cuts, axis=1)

    def lot(q):
        return pl.ds(pl.multiple_of(q * some, some), some)

    pl.semaphore_wait(barrier, n_row + n_col - 2)

    def to_source(k):
        return pltpu.make_async_remote_copy(
            own_source, source_rows.at[row], geo_send.at[0], geo_recv.at[0],
            device_id=(row_at(k), col), device_id_type=MESH)

    def to_receiver(k, other):
        return pltpu.make_async_remote_copy(
            own_receiver, receiver_rows.at[col], geo_send.at[1], geo_recv.at[1],
            device_id=(row, chip_at(k) * 2 + (core + other) % 2), device_id_type=MESH)

    def to_row(u, k):
        return pltpu.make_async_remote_copy(
            own_sent.at[u], gathered.at[u, row], out_send.at[u], out_recv.at[u],
            device_id=(row_at(k), col), device_id_type=MESH)

    def to_pair(u, lot):
        first = pl.ds(lot * (n_chip // 2), n_chip // 2)
        return pltpu.make_async_remote_copy(
            pair_out.at[u, first], pair_in.at[u, first], pair_send.at[u, lot], pair_recv.at[u, lot],
            device_id=(row, chip * 2 + 1 - core), device_id_type=MESH)

    def to_peer(u, k):
        return pltpu.make_async_remote_copy(
            mine.at[u, k], peer_in.at[u, k], peer_send.at[u], peer_recv.at[u],
            device_id=(row, chip_at(k) * 2 + core), device_id_type=MESH)

    def wait_all(like, sem):
        pltpu.make_async_copy(like, like, sem).wait()

    all_source = source_rows.at[pl.ds(0, n_row - 1)]
    all_receiver = receiver_rows.at[pl.ds(0, n_col - 1)]

    def all_row(u):
        return gathered.at[u, pl.ds(0, n_row - 1)]

    def all_peer(u):
        return peer_in.at[u, pl.ds(1, n_chip - 1)]

    for k in range(1, n_chip):
        for other in range(2):
            to_receiver(k, other).start()
    for k in range(1, n_row):
        to_source(k).start()
    to_receiver(0, 1).start()
    source_rows[row] = own_source[...]
    receiver_rows[col] = own_receiver[...]

    fetches[3].wait()
    below = lax.broadcasted_iota(I32, (slots, slots), 0)
    across = lax.broadcasted_iota(I32, (slots, slots), 1)
    code = codes[...]
    lane = lax.broadcasted_iota(I32, (1, slots), 1)
    key = jnp.where(lane < pair_count[0, 0], code, n_source * n_receiver + lane)
    key_across = jnp.broadcast_to(key, (slots, slots))
    key_below = key_across.T
    rank = jnp.sum((key_below < key_across).astype(I32), axis=0, keepdims=True)
    hit = jnp.broadcast_to(rank, (slots, slots)).T == across
    ranked = jnp.sum(jnp.where(hit, key_below, 0), axis=0, keepdims=True)
    receiver = ranked // n_source
    before = jnp.where(lane == 0, -1, pltpu.roll(receiver, 1, 1))
    table[0:1, :] = code
    table[1:2, :] = jnp.sum(jnp.where(hit, below, 0), axis=0, keepdims=True)
    table[2:3, :] = ranked % n_source
    table[3:4, :] = (receiver == before).astype(I32)
    upto = jnp.sum((key_below // n_source <= across).astype(I32), axis=0, keepdims=True)
    table[4:5, :] = jnp.maximum(upto - 1, 0)
    table[5:6, :] = (jnp.sum((key_below // n_source == across).astype(I32), axis=0, keepdims=True) > 0).astype(I32)
    table[6:8, :] = jnp.zeros((2, slots), I32)
    listing = pltpu.make_async_copy(table, ints, table_sem)
    listing.start()

    fetches[4].wait()
    for q in range(PARTS):
        own_sent[q] = shuffled(emission[lot(q), :])
    wait_all(all_source, geo_recv.at[0])

    sub = lax.broadcasted_iota(I32, (8, block), 0)
    turned[...] = jnp.zeros_like(turned)

    def make_left(owner, _):
        for part in range(per_piece):
            h, m, l = pieces(source_rows[owner, :, part * block : (part + 1) * block])
            ones = jnp.where(sub < 3, 1.0, 0.0)
            rows = jnp.concatenate([h, h, m, h, l, m, ones, jnp.zeros((72, block), F32)], axis=0)
            turned[part] = rows.T
            for bit in range(8):
                lhs[owner * per_piece + part, bit * words : (bit + 1) * words, :] = (
                    turned[part, pl.ds(bit, words, stride=8), :].astype(BF16)[:, :64])

        return 0

    lax.fori_loop(0, n_row, make_left, 0, unroll=2)

    for q in range(PARTS):
        for k in range(1, n_row):
            to_row(q, k).start()
    wait_all(all_receiver, geo_recv.at[1])

    def make_right(owner, _):
        for part in range(per_piece):
            x = receiver_rows[owner, :, part * block : (part + 1) * block]
            h, m, l = pieces(x)

            def at(v, row_in, row_out):
                return jnp.where(sub == row_out, pltpu.roll(v, (row_out - row_in) % 8, 0), 0.0)

            def alone(row_in):
                return at(h, row_in, 0) + at(m, row_in, 1) + at(l, row_in, 2)

            zero = jnp.zeros((8, block), F32)
            one_at_7, one_at_3 = jnp.where(sub == 7, 1.0, 0.0), jnp.where(sub == 3, 1.0, 0.0)
            cosine = [jnp.where(sub < 3, v, 0.0) for v in (h, m, l)]
            emitted = [jnp.where((sub > 3) & (sub < 7), v, 0.0) for v in (h, m, l)]
            emitted[0] = emitted[0] + one_at_7
            spread = [jnp.where(sub < 3, pltpu.roll(v, 4, 0) * -2.0, 0.0) for v in (h, m, l)]
            spread[0] = spread[0] + one_at_3
            for n, (v, last) in enumerate(((cosine, alone(3)), (emitted, zero), (spread, alone(7)))):
                full = jnp.concatenate([v[0], v[1], v[0], v[2], v[0], v[1], last, zero], axis=0)
                rhs[owner * per_piece + part, :, n * block : (n + 1) * block] = full.astype(BF16)
        return 0

    lax.fori_loop(0, n_col, make_right, 0, unroll=4)

    fetches[5].wait()
    fetches[6].wait()
    listing.wait()

    def make_factors(step, _):
        for u in range(SLOT_STEP):
            s = step * SLOT_STEP + u
            code = ints[0, s]
            g, h = code // n_source, code % n_source
            for first in range(0, block, CHUNK):
                left = lhs[h, first : first + CHUNK, :]
                met, left_by, spread = (
                    jnp.dot(left, rhs[g, :, n * block : (n + 1) * block], preferred_element_type=F32)
                    for n in range(3))
                bits = range(first // words, (first + CHUNK) // words)
                seen = jnp.concatenate([(seen_words[s] & (1 << bit)) != 0 for bit in bits], axis=0)
                squared = spread * spread
                inverse = pltpu.reciprocal(squared, approx=True)
                value = jnp.maximum(met, 0.0) * jnp.maximum(left_by, 0.0) * inverse
                value = jnp.where(seen, value, 0.0)
                high = value.astype(BF16)
                factor_hi[s, first : first + CHUNK, :] = high
                factor_lo[s, first : first + CHUNK, :] = (value - high.astype(F32)).astype(BF16)
        return 0

    lax.fori_loop(0, slots // SLOT_STEP, make_factors, 0)

    def receive(u):
        q = u % PARTS
        gathered[u, row] = own_sent[u]
        wait_all(all_row(u), out_recv.at[u])

        def split(owner, _):
            for part in range(per_piece):
                x = gathered[u, owner, :, part * block : (part + 1) * block]
                high = x.astype(BF16)
                outgoing[q, owner * per_piece + part, 0:some, :] = high
                outgoing[q, owner * per_piece + part, some : 2 * some, :] = (x - high.astype(F32)).astype(BF16)
            return 0

        lax.fori_loop(0, n_row, split, 0, unroll=True)

    def add_slots(u, first, last, total):
        q = u % PARTS

        def step(n, total):
            for i in range(SWEEP_STEP):
                i = n * SWEEP_STEP + i
                s, h = ints[1, i], ints[2, i]
                left = outgoing[q, h]
                both = jnp.dot(left, factor_hi[s], preferred_element_type=F32)
                fine = jnp.dot(left[:some], factor_lo[s], preferred_element_type=F32)
                total = total * ints[3, i].astype(F32) + (both[:some] + (both[some:] + fine))
                running[q, i] = total
            return total

        return lax.fori_loop(first, last, step, total)

    def summed(q, owner, part):
        g = owner * per_piece + part
        return running[q, ints[4, g]] * ints[5, g].astype(F32)

    order = [k % n_chip for k in range(1, n_chip + 1)]

    def send_pair(u):
        for k in order:
            owner = chip_at(k) * 2 + 1 - core
            for part in range(per_piece):
                pair_out[u, (k - 1) % n_chip, :, part * block : (part + 1) * block] = summed(u % PARTS, owner, part)
            if k == n_chip // 2:
                to_pair(u, 0).start()
        to_pair(u, 1).start()

    def send_peers(u):
        to_pair(u, 0).wait_recv()
        for k in order:
            if k == n_chip // 2 + 1:
                to_pair(u, 1).wait_recv()
            owner = chip_at(k) * 2 + core
            for part in range(per_piece):
                lanes = slice(part * block, (part + 1) * block)
                mine[u, k, :, lanes] = summed(u % PARTS, owner, part) + pair_in[u, (k - 1) % n_chip, :, lanes]
            if k:
                to_peer(u, k).start()

    def gather(u):
        wait_all(all_peer(u), peer_recv.at[u])
        total = mine[u, 0]
        for k in range(1, n_chip):
            total = total + peer_in[u, k]
        return total

    def pass_on(u):
        q = u % PARTS
        own_sent[u + PARTS] = shuffled(emission[lot(q), :] + reflect[lot(q), :] * gather(u))
        for k in range(1, n_row):
            to_row(u + PARTS, k).start()

    steps = slots // SWEEP_STEP
    halves = PARTS * ITERS
    nothing = jnp.zeros((some, block), F32)
    receive(0)
    add_slots(0, 0, steps, nothing)
    send_pair(0)

    def half(u, _):
        send_peers(u - 1)
        receive(u)
        cut = jnp.where(u % PARTS == 0, CUTS[0], CUTS[1])
        total = add_slots(u, 0, cut, nothing)
        pass_on(u - 1)
        add_slots(u, cut, steps, total)
        send_pair(u)
        return 0

    lax.fori_loop(1, halves - 1, half, 0)
    send_peers(halves - 2)
    receive(halves - 1)
    add_slots(halves - 1, 0, steps, nothing)
    send_pair(halves - 1)
    out[lot((halves - 2) % PARTS), :] = gather(halves - 2)
    send_peers(halves - 1)
    out[lot((halves - 1) % PARTS), :] = gather(halves - 1)

    wait_all(all_source, geo_send.at[0])
    wait_all(all_receiver, geo_send.at[1])

    def drain(u, _):
        wait_all(all_row(u), out_send.at[u])
        to_pair(u, 0).wait_send()
        to_pair(u, 1).wait_send()
        wait_all(all_peer(u), peer_send.at[u])
        return 0

    lax.fori_loop(0, halves, drain, 0)


def solution(mesh):
    n_row, n_col = mesh.shape["row"], mesh.shape["col"]

    def body(position, normal, area, emission, reflect, pair_list, pair_count, visible):
        slots, words, block = visible.shape[-3:]
        bands, piece = emission.shape
        per_piece = piece // block
        n_chip = n_col // 2
        n_source, n_receiver = per_piece * n_row, per_piece * n_col
        in_smem = pl.BlockSpec(memory_space=pltpu.SMEM)
        in_vmem = pl.BlockSpec(memory_space=pltpu.VMEM)
        dma = pltpu.SemaphoreType.DMA
        anywhere = pl.BlockSpec(memory_space=pl.ANY)
        some = bands // PARTS
        gathered = pl.pallas_call(
            functools.partial(kernel, n_row, n_col),
            out_shape=jax.ShapeDtypeStruct((bands, piece), F32),
            in_specs=[in_smem] + [anywhere] * 7,
            out_specs=in_vmem,
            scratch_shapes=[
                pltpu.VMEM((slots, block, block), BF16),
                pltpu.VMEM((slots, block, block), BF16),
                pltpu.VMEM((slots, words, block), I32),
                pltpu.VMEM((PARTS, slots, some, block), F32),
                pltpu.VMEM((n_source, block, 64), BF16),
                pltpu.VMEM((n_receiver, 64, 3 * block), BF16),
                pltpu.VMEM((block, block), BF16),
                pltpu.VMEM((per_piece, block, 128), F32),
                pltpu.VMEM((8, piece), F32),
                pltpu.VMEM((8, piece), F32),
                pltpu.VMEM((ITERS * PARTS, some, piece), F32),
                pltpu.VMEM((n_row, 8, piece), F32),
                pltpu.VMEM((n_col, 8, piece), F32),
                pltpu.VMEM((ITERS * PARTS, n_row, some, piece), F32),
                pltpu.VMEM((PARTS, n_source, 2 * some, block), BF16),
                pltpu.VMEM((ITERS * PARTS, n_chip, some, piece), F32),
                pltpu.VMEM((ITERS * PARTS, n_chip, some, piece), F32),
                pltpu.VMEM((ITERS * PARTS, n_chip, some, piece), F32),
                pltpu.VMEM((ITERS * PARTS, n_chip, some, piece), F32),
                pltpu.VMEM((3, piece), F32),
                pltpu.VMEM((3, piece), F32),
                pltpu.VMEM((1, piece), F32),
                pltpu.VMEM((bands, piece), F32),
                pltpu.VMEM((bands, piece), F32),
                pltpu.VMEM((1, slots), I32),
                pltpu.VMEM((8, slots), I32),
                pltpu.SMEM((8, slots), I32),
                dma((7,)),
                dma,
                dma((2,)), dma((2,)),
                dma((ITERS * PARTS,)), dma((ITERS * PARTS,)),
                dma((ITERS * PARTS, 2)), dma((ITERS * PARTS, 2)),
                dma((ITERS * PARTS,)), dma((ITERS * PARTS,)),
            ],
            compiler_params=pltpu.CompilerParams(
                collective_id=0, has_side_effects=True, vmem_limit_bytes=62 * 2**20),
        )(pair_count, pair_list.reshape(1, slots), position, normal, area.reshape(1, piece), emission, reflect,
          visible.reshape(slots, words, block))
        return emission + reflect * gathered

    placed = (
        P(None, ("row", "col")),
        P(None, ("row", "col")),
        P(("row", "col")),
        P(None, ("row", "col")),
        P(None, ("row", "col")),
        P("row", "col", None),
        P("row", "col"),
        P("row", "col", None, None, None),
    )
    return jax.shard_map(
        body, mesh=mesh, in_specs=placed, out_specs=P(None, ("row", "col")), check_vma=False
    )
```
